512 devices in a mesh: row: 64 (over z_hi, y, core), col: 8 (over z_lo, x).
Axes of the slice: x: 4, y: 8, z: 8 (z_hi: 4, z_lo: 2; z = z_hi * 2 + z_lo), core: 2. Of those that a mesh axis runs over, the one named last changes fastest.
Arguments:
- left: bfloat16 [1024, 49152], P('col', 'row'), may hold values from -0.02734375 to 0.02734375
- right: bfloat16 [49152, 4096], P('row', 'col'), may hold values from -6 to 6
- occupancy: int32 [16, 768], P('col', 'row'), may hold values from 0 to 1
- owners: int32 [8], replicated, may hold values from 0 to 7
- slab: bfloat16 [8, 128, 4096], P(None, 'row', 'col'), may hold values from -6 to 6
Outputs:
- updated: float32 [8, 128, 4096], P(None, 'row', 'col')
The draws below stay inside these ranges and needn't reach their ends.
All inputs are finite; a program needn't handle non-finite values.
Results may differ from the reference program's by a relative error of at most 0.0005.
Values may be sent and summed in bfloat16 or wider, within the bound.
No kernel may reach another device: no remote copies, remote signals or barrier semaphores. Data moves between devices by JAX's collectives and lax.ppermute only.
A program may use at most 64 MiB of HBM per device.

```python
import jax
import jax.numpy as jnp
from jax import lax

ATOM_BLOCK = 64
PANEL_ROWS = 128
STEPS = 8
INNER = 49152
COLUMNS = 4096
LEFT_ROWS = 1024
N_COL = 8


def draw_occupancy(key, part):
    key = jax.random.fold_in(key, 5)
    block_rows = LEFT_ROWS // ATOM_BLOCK
    block_cols = INNER // ATOM_BLOCK
    row_ids = jnp.arange(block_rows, dtype=jnp.int32)[:, None]
    col_ids = jnp.arange(block_cols, dtype=jnp.int32)[None, :]
    center = row_ids * block_cols // block_rows
    apart = jnp.abs(col_ids - center)
    apart = jnp.minimum(apart, block_cols - apart)
    banded = apart <= 1
    filled = jax.random.randint(key, (block_rows, block_cols), 0, 16) == 0
    return jnp.where(banded | filled, 1, 0).astype(jnp.int32)


def touch_ends(result, key, low, high):
    dims = result.shape
    index_at = [jax.random.randint(jax.random.fold_in(key, axis), (), 0, dims[axis]) for axis in range(len(dims))]
    result = result.at[tuple(index_at)].set(low)
    longest = dims.index(max(dims))
    index_at[longest] = (index_at[longest] + 1) % dims[longest]
    return result.at[tuple(index_at)].set(high)


def shard_levels(rng, dims, split, smallest, high):
    loudness = 1.0
    for position, shards_of in split:
        heights = jax.random.uniform(jax.random.fold_in(jax.random.fold_in(rng, 6), position), (shards_of,), jnp.float32, smallest / len(split), high / len(split))
        loudness = loudness * jnp.repeat(jnp.exp(heights), dims[position] // shards_of).reshape((-1,) + (1,) * (len(dims) - 1 - position))
    return loudness


def normal_values(own_key, shape, deviation, reach, shards=(), kind=jnp.bfloat16):
    drawn = deviation * jax.random.normal(own_key, shape, jnp.float32)
    if shards:
        drawn = drawn * shard_levels(own_key, shape, shards, -0.22, 0.18)
    return jnp.clip(drawn, -reach, reach).astype(kind)


def setup_inputs(seed: int = 0) -> dict:
    seeds = jax.random.split(jax.random.key(seed), 6)
    left = normal_values(seeds[0], (LEFT_ROWS, INNER), INNER ** -0.5, 0.02734375, ((0, 8), (1, 64)))
    right = normal_values(seeds[1], (INNER, COLUMNS), 1.0, 6.0, ((0, 64), (1, 8)))
    occupancy = draw_occupancy(jax.random.fold_in(seeds[5], 71), 0)
    owners = touch_ends(jax.random.randint(seeds[3], (STEPS,), 0, N_COL), jax.random.fold_in(seeds[3], 1), 0, N_COL - 1).astype(jnp.int32)
    slab = normal_values(seeds[4], (STEPS, PANEL_ROWS, COLUMNS), 1.0, 6.0, ((1, 64), (2, 8)))
    return {"left": left, "right": right, "occupancy": occupancy, "owners": owners, "slab": slab}


def reference(left, right, occupancy, owners, slab):
    marks = occupancy.astype(jnp.bfloat16)
    count_r, count_c = marks.shape
    expanded = jnp.broadcast_to(marks[:, None, :, None], (count_r, ATOM_BLOCK, count_c, ATOM_BLOCK)).reshape(count_r * ATOM_BLOCK, count_c * ATOM_BLOCK)
    kept = left * expanded
    results = []
    for step in range(STEPS):
        start = (owners[step] * PANEL_ROWS).astype(jnp.int32)
        panel = lax.dynamic_slice_in_dim(kept, start, PANEL_ROWS, 0)
        product = jnp.dot(panel, right, preferred_element_type=jnp.float32)
        results.append(1.5 * slab[step].astype(jnp.float32) - 0.5 * product)
    return jnp.stack(results)
```

```python
import jax
import jax.numpy as jnp
from jax import lax
from jax.sharding import Mesh, PartitionSpec as P

ATOM_BLOCK = 64
STEPS = 8
PANEL_ROWS = 128
WIRE = jnp.float16
WIRE_SCALE_Y = 128.0
WIRE_SCALE_Z = 16.0


def shift(value, axis, count, by):
    return lax.ppermute(value, axis, [(i, (i + by) % count) for i in range(count)])


def row_order(y, zhi, core):
    place = lax.broadcasted_iota(jnp.int32, (64, PANEL_ROWS), 0)
    row = lax.broadcasted_iota(jnp.int32, (64, PANEL_ROWS), 1)
    s, u, b = place // 8, (place // 2) % 4, place % 2
    wanted = ((zhi + u) % 4) * 32 + ((y + s) % 8) * 4 + core * 2 + b
    return (row == wanted).astype(jnp.bfloat16)


def spread_marks(marks):
    values = marks.astype(jnp.bfloat16)
    count_r, count_c = values.shape
    return jnp.broadcast_to(
        values[:, None, :, None], (count_r, ATOM_BLOCK, count_c, ATOM_BLOCK)
    ).reshape(count_r * ATOM_BLOCK, count_c * ATOM_BLOCK)


def body(left, right, occupancy, owners, slab):
    zhi, y, core = (lax.axis_index(a) for a in ("zhi", "y", "core"))
    zlo, x = lax.axis_index("zlo"), lax.axis_index("x")

    depth, width = right.shape

    kept = left * spread_marks(occupancy)

    def pick(which):
        return jnp.dot(row_order(y, zhi, which), kept, preferred_element_type=jnp.float32).astype(jnp.bfloat16)

    right2 = shift(right, "core", 2, 1)
    mine = jnp.concatenate([pick(core), shift(pick(1 - core), "core", 2, 1)], axis=1)

    def ring(panel):
        from_left = shift(panel, "x", 4, 1)
        from_right = shift(panel, "x", 4, -1)
        far = jnp.concatenate(
            [shift(from_left[:32], "x", 4, 1), shift(from_right[32:], "x", 4, -1)], axis=0
        )
        return [panel, from_right, far, from_left]

    panels = ring(mine) + ring(shift(mine, "zlo", 2, 1))

    products = []
    for panel in panels:
        products.append(
            jnp.dot(panel[:, :depth], right, preferred_element_type=jnp.float32)
            + jnp.dot(panel[:, depth:], right2, preferred_element_type=jnp.float32)
        )
    product = jnp.stack(products).reshape(8, 8, 8, width)

    total = product[:, 0]
    for s in range(1, 8):
        got = shift((product[:, s] * WIRE_SCALE_Y).astype(WIRE), "y", 8, s)
        total = total + got.astype(jnp.float32) * (1.0 / WIRE_SCALE_Y)

    parts = total.reshape(8, 4, 2, width)
    summed = parts[:, 0]
    for u in range(1, 4):
        got = shift((parts[:, u] * WIRE_SCALE_Z).astype(WIRE), "zhi", 4, u)
        summed = summed + got.astype(jnp.float32) * (1.0 / WIRE_SCALE_Z)

    place = ((owners // 4) ^ zlo) * 4 + (owners % 4 - x) % 4
    chosen = place[:, None] == jnp.arange(8)[None, :]
    picked = jnp.sum(jnp.where(chosen[:, :, None, None], summed[None], 0.0), axis=1)
    return 1.5 * slab.astype(jnp.float32) - 0.5 * picked


def solution(mesh):
    fine = Mesh(mesh.devices.reshape(4, 8, 2, 2, 4), ("zhi", "y", "core", "zlo", "x"))
    row, col = ("zhi", "y", "core"), ("zlo", "x")
    in_specs = (P(col, row), P(row, col), P(col, row), P(), P(None, row, col))
    out_specs = P(None, row, col)
    return jax.shard_map(body, mesh=fine, in_specs=in_specs, out_specs=out_specs, check_vma=False)
```

```python
import jax
import jax.numpy as jnp
from jax import lax
from jax.sharding import Mesh, PartitionSpec as P

ATOM_BLOCK = 64
PANEL_ROWS = 128
WIRE_SCALE = 2.0**18


def row_order():
    place = lax.broadcasted_iota(jnp.int32, (PANEL_ROWS, PANEL_ROWS), 0)
    row = lax.broadcasted_iota(jnp.int32, (PANEL_ROWS, PANEL_ROWS), 1)
    core, at, b = place // 64, (place % 64) // 2, place % 2
    return (row == at * 4 + core * 2 + b).astype(jnp.bfloat16)


def spread_marks(marks):
    values = marks.astype(jnp.bfloat16)
    count_r, count_c = values.shape
    return jnp.broadcast_to(
        values[:, None, :, None], (count_r, ATOM_BLOCK, count_c, ATOM_BLOCK)
    ).reshape(count_r * ATOM_BLOCK, count_c * ATOM_BLOCK)


def body(left, right, occupancy, owners, slab):
    core = lax.axis_index("core")
    depth, width = right.shape

    right2 = lax.ppermute(right, "core", [(0, 1), (1, 0)])

    kept = left * spread_marks(occupancy)
    halves = jnp.dot(row_order(), kept, preferred_element_type=jnp.float32).astype(jnp.bfloat16)
    sent = jnp.broadcast_to(halves.reshape(2, 1, 64, depth), (2, 8, 64, depth)).reshape(16, 64, depth)
    panels = lax.all_to_all(sent, ("core", "zlo", "x"), 0, 0, tiled=True).reshape(2, 512, depth)

    own = lax.dynamic_index_in_dim(panels, core, 0, keepdims=False)
    other = lax.dynamic_index_in_dim(panels, 1 - core, 0, keepdims=False)
    product = jnp.dot(own, right, preferred_element_type=jnp.float32) + jnp.dot(
        other, right2, preferred_element_type=jnp.float32
    )

    parts = jnp.round(product * WIRE_SCALE).astype(jnp.int32).reshape(8, 32, 2, width).transpose(1, 0, 2, 3).reshape(32, 16, width)
    total = lax.psum_scatter(parts, ("zhi", "y"), scatter_dimension=0, tiled=True)
    summed = total.astype(jnp.float32).reshape(8, 2, width) * (1.0 / WIRE_SCALE)

    chosen = owners[:, None] == jnp.arange(8)[None, :]
    picked = jnp.sum(jnp.where(chosen[:, :, None, None], summed[None], 0.0), axis=1)
    return 1.5 * slab.astype(jnp.float32) - 0.5 * picked


def solution(mesh):
    fine = Mesh(mesh.devices.reshape(4, 8, 2, 2, 4), ("zhi", "y", "core", "zlo", "x"))
    row, col = ("zhi", "y", "core"), ("zlo", "x")
    in_specs = (P(col, row), P(row, col), P(col, row), P(), P(None, row, col))
    out_specs = P(None, row, col)
    return jax.shard_map(body, mesh=fine, in_specs=in_specs, out_specs=out_specs, check_vma=False)
```

```python
import jax
import jax.numpy as jnp
from jax import lax
from jax.experimental import pallas as pl
from jax.experimental.pallas import tpu as pltpu
from jax.sharding import Mesh, PartitionSpec as P

ATOM_BLOCK = 64
PANEL_ROWS = 128
HALF = 64
SLOTS = 8
LANES = 128
PACKED_ROWS = SLOTS // 2 * 32
LIST_ROWS = 16
WIRE = jnp.float16
WIRE_SCALE = 128.0


def row_order():
    place = lax.broadcasted_iota(jnp.int32, (PANEL_ROWS, PANEL_ROWS), 0)
    row = lax.broadcasted_iota(jnp.int32, (PANEL_ROWS, PANEL_ROWS), 1)
    core, at, b = place // HALF, (place % HALF) // 2, place % 2
    return (row == at * 4 + core * 2 + b).astype(jnp.bfloat16)


def pack_kernel(marks_ref, left_ref, out_ref, rows, tiles):
    rows[...] = jnp.dot(row_order(), left_ref[...], preferred_element_type=jnp.float32).astype(jnp.bfloat16)
    tiles[...] = jnp.zeros_like(tiles)
    lane = lax.broadcasted_iota(jnp.int32, (32, LANES), 1)
    list_lane = lax.broadcasted_iota(jnp.int32, (LIST_ROWS, LANES), 1)
    block_rows, block_cols = marks_ref.shape
    count = jnp.int32(0)
    listed = jnp.zeros((LIST_ROWS, LANES), jnp.float32)
    for i in range(block_rows):
        for j in range(block_cols):
            kept = marks_ref[i, j] != 0
            slot = jnp.minimum(count, SLOTS - 1)
            fits = jnp.logical_and(kept, count < SLOTS)

            @pl.when(fits)
            def _(i=i, j=j, slot=slot):
                side = lax.rem(slot, 2)
                here = lane // ATOM_BLOCK == side
                at = pl.ds(pl.multiple_of(lax.div(slot, 2) * 32, 32), 32)
                for half in range(2):
                    block = rows[half * HALF + i * 32 : half * HALF + i * 32 + 32, j // 2 * LANES : (j // 2 + 1) * LANES]
                    turned = pltpu.roll(block, ATOM_BLOCK, 1)
                    placed = jnp.where(side == j % 2, block, turned)
                    tiles[half, at, :] = jnp.where(here, placed, tiles[half, at, :])

            mark = jnp.where(fits, 1.0, 0.0)
            listed = listed + jnp.where(list_lane == slot, mark * i, 0.0)
            listed = listed + jnp.where(list_lane == slot + 16, mark * j, 0.0)
            count = count + kept.astype(jnp.int32)
    listed = listed + jnp.where(list_lane == 32, count.astype(jnp.float32), 0.0)
    for to in range(out_ref.shape[0]):
        out_ref[to, :PACKED_ROWS, :] = tiles[to // 8]
        out_ref[to, PACKED_ROWS:, :] = listed.astype(jnp.bfloat16)


def product_kernel(core_ref, got_ref, right_ref, right2_ref, out_ref, dense, lists, places, sem):
    sources = got_ref.shape[0]
    depth = right_ref.shape[0]
    core = core_ref[0]
    for source in range(sources):
        lists[source * 8 : source * 8 + 8, :] = got_ref[source, PACKED_ROWS:, :].astype(jnp.int32)[:8]
    copy = pltpu.make_async_copy(lists, places, sem)
    copy.start()
    dense[...] = jnp.zeros_like(dense)
    copy.wait()
    lane = lax.broadcasted_iota(jnp.int32, (32, LANES), 1)

    def one_source(source, too_many):
        count = places[source * 8, 32]
        first = jnp.where(source // 8 == core, 0, depth)
        top = lax.rem(source, 8) * HALF

        def one_block(slot, carry):
            i = places[source * 8, slot]
            j = places[source * 8, slot + 16]
            block = got_ref[source, pl.ds(pl.multiple_of(lax.div(slot, 2) * 32, 32), 32), :]
            side = lax.rem(j, 2)
            placed = jnp.where(side == lax.rem(slot, 2), block, pltpu.roll(block, ATOM_BLOCK, 1))
            to_rows = pl.ds(pl.multiple_of(top + i * 32, 32), 32)
            to_lanes = pl.ds(pl.multiple_of(first + lax.div(j, 2) * LANES, LANES), LANES)
            dense[to_rows, to_lanes] = jnp.where(lane // ATOM_BLOCK == side, placed, dense[to_rows, to_lanes])
            return carry

        lax.fori_loop(0, jnp.minimum(count, SLOTS), one_block, 0)
        return jnp.logical_or(too_many, count > SLOTS)

    too_many = lax.fori_loop(0, sources, one_source, jnp.bool_(False))
    for m in range(0, out_ref.shape[0], 128):
        out_ref[m : m + 128, :] = jnp.dot(
            dense[m : m + 128, :depth], right_ref[...], preferred_element_type=jnp.float32
        ) + jnp.dot(dense[m : m + 128, depth:], right2_ref[...], preferred_element_type=jnp.float32)

    @pl.when(too_many)
    def _():
        out_ref[...] = jnp.full(out_ref.shape, jnp.nan, jnp.float32)


def pack(marks, left):
    return pl.pallas_call(
        pack_kernel,
        out_shape=jax.ShapeDtypeStruct((16, PACKED_ROWS + LIST_ROWS, LANES), jnp.bfloat16),
        in_specs=[pl.BlockSpec(memory_space=pltpu.SMEM), pl.BlockSpec(memory_space=pltpu.VMEM)],
        out_specs=pl.BlockSpec(memory_space=pltpu.VMEM),
        scratch_shapes=[
            pltpu.VMEM(left.shape, jnp.bfloat16),
            pltpu.VMEM((2, PACKED_ROWS, LANES), jnp.bfloat16),
        ],
    )(marks, left)


def unpack_product(core, got, right, right2):
    depth, width = right.shape
    return pl.pallas_call(
        product_kernel,
        out_shape=jax.ShapeDtypeStruct((8 * HALF, width), jnp.float32),
        in_specs=[pl.BlockSpec(memory_space=pltpu.SMEM)] + [pl.BlockSpec(memory_space=pltpu.VMEM)] * 3,
        out_specs=pl.BlockSpec(memory_space=pltpu.VMEM),
        scratch_shapes=[
            pltpu.VMEM((8 * HALF, 2 * depth), jnp.bfloat16),
            pltpu.VMEM((16 * 8, LANES), jnp.int32),
            pltpu.SMEM((16 * 8, LANES), jnp.int32),
            pltpu.SemaphoreType.DMA,
        ],
        compiler_params=pltpu.CompilerParams(vmem_limit_bytes=24 * 2**20),
        cost_estimate=pl.CostEstimate(flops=2 * 8 * HALF * 2 * depth * width, bytes_accessed=4 * 2**20, transcendentals=0),
    )(core.reshape(1), got, right, right2)


def spread_marks(marks):
    values = marks.astype(jnp.bfloat16)
    count_r, count_c = values.shape
    return jnp.broadcast_to(
        values[:, None, :, None], (count_r, ATOM_BLOCK, count_c, ATOM_BLOCK)
    ).reshape(count_r * ATOM_BLOCK, count_c * ATOM_BLOCK)


def dense_product(core, left, right, right2, occupancy):
    depth = right.shape[0]
    kept = left * spread_marks(occupancy)
    halves = jnp.dot(row_order(), kept, preferred_element_type=jnp.float32).astype(jnp.bfloat16)
    sent = jnp.broadcast_to(halves.reshape(2, 1, HALF, depth), (2, 8, HALF, depth)).reshape(16, HALF, depth)
    panels = lax.all_to_all(sent, ("core", "zlo", "x"), 0, 0, tiled=True).reshape(2, 8 * HALF, depth)
    own = lax.dynamic_index_in_dim(panels, core, 0, keepdims=False)
    other = lax.dynamic_index_in_dim(panels, 1 - core, 0, keepdims=False)
    return jnp.dot(own, right, preferred_element_type=jnp.float32) + jnp.dot(
        other, right2, preferred_element_type=jnp.float32
    )


def reduce_rows(product):
    width = product.shape[-1]
    parts = (product * WIRE_SCALE).astype(WIRE).reshape(8, 32, 2, width).transpose(1, 0, 2, 3)
    got = lax.all_to_all(parts, ("zhi", "y"), 0, 0, tiled=True)
    return jnp.sum(got.astype(jnp.float32), axis=0) * (1.0 / WIRE_SCALE)


def body(left, right, occupancy, owners, slab):
    core = lax.axis_index("core")

    right2 = lax.ppermute(right, "core", [(0, 1), (1, 0)])

    got = lax.all_to_all(pack(occupancy, left), ("core", "zlo", "x"), 0, 0, tiled=True)
    summed = reduce_rows(unpack_product(core, got, right, right2))

    summed = lax.cond(
        jnp.isnan(summed[0, 0, 0]),
        lambda: reduce_rows(dense_product(core, left, right, right2, occupancy)),
        lambda: summed,
    )

    chosen = owners[:, None] == jnp.arange(8)[None, :]
    picked = jnp.sum(jnp.where(chosen[:, :, None, None], summed[None], 0.0), axis=1)
    return 1.5 * slab.astype(jnp.float32) - 0.5 * picked


def solution(mesh):
    fine = Mesh(mesh.devices.reshape(4, 8, 2, 2, 4), ("zhi", "y", "core", "zlo", "x"))
    row, col = ("zhi", "y", "core"), ("zlo", "x")
    in_specs = (P(col, row), P(row, col), P(col, row), P(), P(None, row, col))
    out_specs = P(None, row, col)
    return jax.shard_map(body, mesh=fine, in_specs=in_specs, out_specs=out_specs, check_vma=False)
```

```python
import jax
import jax.numpy as jnp
from jax import lax
from jax.experimental import pallas as pl
from jax.experimental.pallas import tpu as pltpu
from jax.sharding import Mesh, PartitionSpec as P

ATOM_BLOCK = 64
PANEL_ROWS = 128
HALF = 64
SLOTS = 8
LANES = 128
PACKED_ROWS = SLOTS // 2 * 32
LIST_ROWS = 16
WIRE = jnp.float16
WIRE_SCALE = 128.0
PAIR_SCALE = 64.0


def row_order():
    place = lax.broadcasted_iota(jnp.int32, (PANEL_ROWS, PANEL_ROWS), 0)
    row = lax.broadcasted_iota(jnp.int32, (PANEL_ROWS, PANEL_ROWS), 1)
    core, at, b = place // HALF, (place % HALF) // 2, place % 2
    return (row == at * 4 + core * 2 + b).astype(jnp.bfloat16)


def pack_kernel(marks_ref, left_ref, out_ref, rows, tiles):
    rows[...] = jnp.dot(row_order(), left_ref[...], preferred_element_type=jnp.float32).astype(jnp.bfloat16)
    tiles[...] = jnp.zeros_like(tiles)
    lane = lax.broadcasted_iota(jnp.int32, (32, LANES), 1)
    list_lane = lax.broadcasted_iota(jnp.int32, (LIST_ROWS, LANES), 1)
    block_rows, block_cols = marks_ref.shape
    count = jnp.int32(0)
    listed = jnp.zeros((LIST_ROWS, LANES), jnp.float32)
    for i in range(block_rows):
        for j in range(block_cols):
            kept = marks_ref[i, j] != 0
            slot = jnp.minimum(count, SLOTS - 1)
            fits = jnp.logical_and(kept, count < SLOTS)

            @pl.when(fits)
            def _(i=i, j=j, slot=slot):
                side = lax.rem(slot, 2)
                here = lane // ATOM_BLOCK == side
                at = pl.ds(pl.multiple_of(lax.div(slot, 2) * 32, 32), 32)
                for half in range(2):
                    block = rows[half * HALF + i * 32 : half * HALF + i * 32 + 32, j // 2 * LANES : (j // 2 + 1) * LANES]
                    turned = pltpu.roll(block, ATOM_BLOCK, 1)
                    placed = jnp.where(side == j % 2, block, turned)
                    tiles[half, at, :] = jnp.where(here, placed, tiles[half, at, :])

            mark = jnp.where(fits, 1.0, 0.0)
            listed = listed + jnp.where(list_lane == slot, mark * i, 0.0)
            listed = listed + jnp.where(list_lane == slot + 16, mark * j, 0.0)
            count = count + kept.astype(jnp.int32)
    listed = listed + jnp.where(list_lane == 32, count.astype(jnp.float32), 0.0)
    for to in range(out_ref.shape[0]):
        out_ref[to, :PACKED_ROWS, :] = tiles[to // 8]
        out_ref[to, PACKED_ROWS:, :] = listed.astype(jnp.bfloat16)


def destination_order(parity):
    place = lax.broadcasted_iota(jnp.int32, (256, 256), 0)
    row = lax.broadcasted_iota(jnp.int32, (256, 256), 1)
    away, zhi, pair, panel, b = place // 128, place // 64 % 2, place // 16 % 4, place // 2 % 8, place % 2
    y = 2 * pair + (parity + away) % 2
    return (row == panel * 32 + zhi * 16 + y * 2 + b).astype(jnp.bfloat16)


def product_kernel(at_ref, got_ref, right_ref, right2_ref, keep_ref, send_ref, dense, lists, places, sem):
    sources = got_ref.shape[0]
    depth = right_ref.shape[0]
    core, parity = at_ref[0], at_ref[1]
    for source in range(sources):
        lists[source : source + 1, :] = got_ref[source, PACKED_ROWS : PACKED_ROWS + 1, :].astype(jnp.int32)
    copy = pltpu.make_async_copy(lists, places, sem)
    copy.start()
    dense[...] = jnp.zeros_like(dense)
    copy.wait()
    lane = lax.broadcasted_iota(jnp.int32, (32, LANES), 1)

    def one_source(source, too_many):
        count = places[source, 32]
        first = jnp.where(lax.div(source, 8) == core, 0, depth)
        panel = lax.rem(source, 8) * 32

        def one_block(slot, carry):
            i = places[source, slot]
            j = places[source, slot + 16]
            block = got_ref[source, pl.ds(pl.multiple_of(lax.div(slot, 2) * 32, 32), 32), :]
            side = lax.rem(j, 2)
            placed = jnp.where(side == lax.rem(slot, 2), block, pltpu.roll(block, ATOM_BLOCK, 1))
            to_rows = pl.ds(pl.multiple_of(i * 256 + panel, 32), 32)
            to_lanes = pl.ds(pl.multiple_of(first + lax.div(j, 2) * LANES, LANES), LANES)
            dense[to_rows, to_lanes] = jnp.where(lane // ATOM_BLOCK == side, placed, dense[to_rows, to_lanes])
            return carry

        lax.fori_loop(0, jnp.minimum(count, SLOTS), one_block, 0)
        return jnp.logical_or(too_many, count > SLOTS)

    too_many = lax.fori_loop(0, sources, one_source, jnp.bool_(False))
    order = destination_order(parity)
    for i in range(2):
        rows = jnp.dot(order, dense[i * 256 : i * 256 + 256, :], preferred_element_type=jnp.float32).astype(jnp.bfloat16)
        sums = jnp.dot(rows[:, :depth], right_ref[...], preferred_element_type=jnp.float32) + jnp.dot(
            rows[:, depth:], right2_ref[...], preferred_element_type=jnp.float32
        )
        keep_ref[i * 128 : i * 128 + 128, :] = sums[:128]
        send_ref[i * 128 : i * 128 + 128, :] = sums[128:]

    @pl.when(too_many)
    def _():
        keep_ref[...] = jnp.full(keep_ref.shape, jnp.nan, jnp.float32)
        send_ref[...] = jnp.full(send_ref.shape, jnp.nan, jnp.float32)


def pack(marks, left):
    return pl.pallas_call(
        pack_kernel,
        out_shape=jax.ShapeDtypeStruct((16, PACKED_ROWS + LIST_ROWS, LANES), jnp.bfloat16),
        in_specs=[pl.BlockSpec(memory_space=pltpu.SMEM), pl.BlockSpec(memory_space=pltpu.VMEM)],
        out_specs=pl.BlockSpec(memory_space=pltpu.VMEM),
        scratch_shapes=[
            pltpu.VMEM(left.shape, jnp.bfloat16),
            pltpu.VMEM((2, PACKED_ROWS, LANES), jnp.bfloat16),
        ],
    )(marks, left)


def unpack_product(core, parity, got, right, right2):
    depth, width = right.shape
    return pl.pallas_call(
        product_kernel,
        out_shape=[jax.ShapeDtypeStruct((256, width), jnp.float32)] * 2,
        in_specs=[pl.BlockSpec(memory_space=pltpu.SMEM)] + [pl.BlockSpec(memory_space=pltpu.VMEM)] * 3,
        out_specs=[pl.BlockSpec(memory_space=pltpu.VMEM)] * 2,
        scratch_shapes=[
            pltpu.VMEM((512, 2 * depth), jnp.bfloat16),
            pltpu.VMEM((16, LANES), jnp.int32),
            pltpu.SMEM((16, LANES), jnp.int32),
            pltpu.SemaphoreType.DMA,
        ],
        compiler_params=pltpu.CompilerParams(vmem_limit_bytes=24 * 2**20),
        cost_estimate=pl.CostEstimate(flops=2 * 512 * 2 * depth * width, bytes_accessed=4 * 2**20, transcendentals=0),
    )(jnp.stack([core, parity]), got, right, right2)


def spread_marks(marks):
    values = marks.astype(jnp.bfloat16)
    count_r, count_c = values.shape
    return jnp.broadcast_to(
        values[:, None, :, None], (count_r, ATOM_BLOCK, count_c, ATOM_BLOCK)
    ).reshape(count_r * ATOM_BLOCK, count_c * ATOM_BLOCK)


def dense_product(core, left, right, right2, occupancy):
    depth = right.shape[0]
    kept = left * spread_marks(occupancy)
    halves = jnp.dot(row_order(), kept, preferred_element_type=jnp.float32).astype(jnp.bfloat16)
    sent = jnp.broadcast_to(halves.reshape(2, 1, HALF, depth), (2, 8, HALF, depth)).reshape(16, HALF, depth)
    panels = lax.all_to_all(sent, ("core", "zlo", "x"), 0, 0, tiled=True).reshape(2, 8 * HALF, depth)
    own = lax.dynamic_index_in_dim(panels, core, 0, keepdims=False)
    other = lax.dynamic_index_in_dim(panels, 1 - core, 0, keepdims=False)
    return jnp.dot(own, right, preferred_element_type=jnp.float32) + jnp.dot(
        other, right2, preferred_element_type=jnp.float32
    )


def reduce_dense(product):
    width = product.shape[-1]
    parts = (product * WIRE_SCALE).astype(WIRE).reshape(8, 32, 2, width).transpose(1, 0, 2, 3)
    got = lax.all_to_all(parts, ("zhi", "pair", "parity"), 0, 0, tiled=True)
    return jnp.sum(got.astype(jnp.float32), axis=0) * (1.0 / WIRE_SCALE)


def reduce_rows(keep, send):
    width = keep.shape[-1]
    came = lax.ppermute((send * WIRE_SCALE).astype(WIRE), "parity", [(0, 1), (1, 0)])
    total = keep + came.astype(jnp.float32) * (1.0 / WIRE_SCALE)
    parts = (total * PAIR_SCALE).astype(WIRE).reshape(16, 16, width)
    got = lax.all_to_all(parts, ("zhi", "pair"), 0, 0, tiled=True)
    return (jnp.sum(got.astype(jnp.float32), axis=0) * (1.0 / PAIR_SCALE)).reshape(8, 2, width)


def body(left, right, occupancy, owners, slab):
    core, parity = lax.axis_index("core"), lax.axis_index("parity")

    right2 = lax.ppermute(right, "core", [(0, 1), (1, 0)])

    got = lax.all_to_all(pack(occupancy, left), ("core", "zlo", "x"), 0, 0, tiled=True)
    summed = reduce_rows(*unpack_product(core, parity, got, right, right2))

    summed = lax.cond(
        jnp.isnan(summed[0, 0, 0]),
        lambda: reduce_dense(dense_product(core, left, right, right2, occupancy)),
        lambda: summed,
    )

    chosen = owners[:, None] == jnp.arange(8)[None, :]
    picked = jnp.sum(jnp.where(chosen[:, :, None, None], summed[None], 0.0), axis=1)
    return 1.5 * slab.astype(jnp.float32) - 0.5 * picked


def solution(mesh):
    fine = Mesh(mesh.devices.reshape(4, 4, 2, 2, 2, 4), ("zhi", "pair", "parity", "core", "zlo", "x"))
    row, col = ("zhi", "pair", "parity", "core"), ("zlo", "x")
    in_specs = (P(col, row), P(row, col), P(col, row), P(), P(None, row, col))
    out_specs = P(None, row, col)
    return jax.shard_map(body, mesh=fine, in_specs=in_specs, out_specs=out_specs, check_vma=False)
```

```python
import functools

import jax
import jax.numpy as jnp
from jax import lax
from jax.experimental import pallas as pl
from jax.experimental.pallas import tpu as pltpu
from jax.sharding import Mesh, PartitionSpec as P

ATOM_BLOCK = 64
PANEL_ROWS = 128
HALF = 64
SLOTS = 8
LANES = 128
TILE = 8
DISTINCT = (4, 5, 6, 8)
PACKED_ROWS = SLOTS // 2 * 32
LIST_ROWS = 16
WIRE = jnp.float16
WIRE_SCALE = 128.0


def row_order():
    place = lax.broadcasted_iota(jnp.int32, (PANEL_ROWS, PANEL_ROWS), 0)
    row = lax.broadcasted_iota(jnp.int32, (PANEL_ROWS, PANEL_ROWS), 1)
    core, at, b = place // HALF, (place % HALF) // 2, place % 2
    return (row == at * 4 + core * 2 + b).astype(jnp.bfloat16)


def pack_kernel(marks_ref, left_ref, out_ref, rows, tiles):
    rows[...] = jnp.dot(row_order(), left_ref[...], preferred_element_type=jnp.float32).astype(jnp.bfloat16)
    tiles[...] = jnp.zeros_like(tiles)
    lane = lax.broadcasted_iota(jnp.int32, (32, LANES), 1)
    list_lane = lax.broadcasted_iota(jnp.int32, (LIST_ROWS, LANES), 1)
    block_rows, block_cols = marks_ref.shape
    count = jnp.int32(0)
    listed = jnp.zeros((LIST_ROWS, LANES), jnp.float32)
    for i in range(block_rows):
        for j in range(block_cols):
            kept = marks_ref[i, j] != 0
            slot = jnp.minimum(count, SLOTS - 1)
            fits = jnp.logical_and(kept, count < SLOTS)

            @pl.when(fits)
            def _(i=i, j=j, slot=slot):
                side = lax.rem(slot, 2)
                here = lane // ATOM_BLOCK == side
                at = pl.ds(pl.multiple_of(lax.div(slot, 2) * 32, 32), 32)
                for half in range(2):
                    block = rows[half * HALF + i * 32 : half * HALF + i * 32 + 32, j // 2 * LANES : (j // 2 + 1) * LANES]
                    turned = pltpu.roll(block, ATOM_BLOCK, 1)
                    placed = jnp.where(side == j % 2, block, turned)
                    tiles[half, at, :] = jnp.where(here, placed, tiles[half, at, :])

            mark = jnp.where(fits, 1.0, 0.0)
            listed = listed + jnp.where(list_lane == slot, mark * i, 0.0)
            listed = listed + jnp.where(list_lane == slot + 16, mark * j, 0.0)
            count = count + kept.astype(jnp.int32)
    listed = listed + jnp.where(list_lane == 32, count.astype(jnp.float32), 0.0)
    for to in range(out_ref.shape[0]):
        out_ref[to, :PACKED_ROWS, :] = tiles[to // 8]
        out_ref[to, PACKED_ROWS:, :] = listed.astype(jnp.bfloat16)


def destination_order(owners_ref, slots):
    shape = (32 * slots, 256)
    place = lax.broadcasted_iota(jnp.int32, shape, 0)
    row = lax.broadcasted_iota(jnp.int32, shape, 1)
    at, slot, b = place // (2 * slots), place // 2 % slots, place % 2
    wanted = at * 2 + b
    filled = jnp.int32(0)
    for panel in range(8):
        owned = functools.reduce(jnp.logical_or, [owners_ref[t] == panel for t in range(owners_ref.shape[0])])
        wanted = wanted + jnp.where(slot == jnp.where(owned, filled, slots), panel * 32, 0)
        filled = filled + owned.astype(jnp.int32)
    return (row == wanted).astype(jnp.bfloat16)


def product_kernel(slots, core_ref, owners_ref, got_ref, right_ref, right2_ref, out_ref, dense, lists, places, sem):
    sources = got_ref.shape[0]
    depth = right_ref.shape[0]
    core = core_ref[0]
    for source in range(sources):
        lists[source : source + 1, :] = got_ref[source, PACKED_ROWS : PACKED_ROWS + 1, :].astype(jnp.int32)
    copy = pltpu.make_async_copy(lists, places, sem)
    copy.start()
    dense[...] = jnp.zeros_like(dense)
    order = destination_order(owners_ref, slots)
    copy.wait()
    side_of_lane = lax.broadcasted_iota(jnp.int32, (32, LANES), 1) // ATOM_BLOCK

    def put(source, first, slots_here):
        for slot in slots_here:
            i = places[source, slot]
            j = places[source, slot + 16]
            block = got_ref[source, slot // 2 * 32 : slot // 2 * 32 + 32, :]
            turned = pltpu.roll(block, ATOM_BLOCK, 1)
            side = lax.rem(j, 2)
            placed = jnp.where(side == slot % 2, block, turned)
            to_rows = pl.ds(pl.multiple_of(i * 256 + source % 8 * 32, 32), 32)
            to_lanes = pl.ds(pl.multiple_of(first + lax.div(j, 2) * LANES, LANES), LANES)
            here = side_of_lane == jnp.where(slot < places[source, 32], side, 2)
            dense[to_rows, to_lanes] = jnp.where(here, placed, dense[to_rows, to_lanes])

    too_many = jnp.bool_(False)
    for source in range(sources):
        first = jnp.where(core == source // 8, 0, depth)
        put(source, first, range(SLOTS // 2))

        @pl.when(places[source, 32] > SLOTS // 2)
        def _(source=source, first=first):
            put(source, first, range(SLOTS // 2, SLOTS))

        too_many = jnp.logical_or(too_many, places[source, 32] > SLOTS)

    size = 32 * slots
    for i in range(2):
        rows = jnp.dot(order, dense[i * 256 : i * 256 + 256, :], preferred_element_type=jnp.float32).astype(jnp.bfloat16)
        sums = jnp.dot(rows[:, :depth], right_ref[...], preferred_element_type=jnp.float32) + jnp.dot(
            rows[:, depth:], right2_ref[...], preferred_element_type=jnp.float32
        )
        parts = sums.shape[1] // LANES
        for q in range(parts):
            out_ref[pl.ds(i * size * parts + q, size, stride=parts), :] = sums[:, q * LANES : (q + 1) * LANES]

    @pl.when(too_many)
    def _():
        out_ref[...] = jnp.full(out_ref.shape, jnp.nan, jnp.float32)


def pack(marks, left):
    return pl.pallas_call(
        pack_kernel,
        out_shape=jax.ShapeDtypeStruct((16, PACKED_ROWS + LIST_ROWS, LANES), jnp.bfloat16),
        in_specs=[pl.BlockSpec(memory_space=pltpu.SMEM), pl.BlockSpec(memory_space=pltpu.VMEM)],
        out_specs=pl.BlockSpec(memory_space=pltpu.VMEM),
        scratch_shapes=[
            pltpu.VMEM(left.shape, jnp.bfloat16),
            pltpu.VMEM((2, PACKED_ROWS, LANES), jnp.bfloat16),
        ],
    )(marks, left)


def unpack_product(slots, core, owners, got, right, right2):
    depth, width = right.shape
    return pl.pallas_call(
        functools.partial(product_kernel, slots),
        out_shape=jax.ShapeDtypeStruct((32 * slots * 2 * (width // LANES), LANES), jnp.float32),
        in_specs=[pl.BlockSpec(memory_space=pltpu.SMEM)] * 2 + [pl.BlockSpec(memory_space=pltpu.VMEM)] * 3,
        out_specs=pl.BlockSpec(memory_space=pltpu.VMEM),
        scratch_shapes=[
            pltpu.VMEM((512, 2 * depth), jnp.bfloat16),
            pltpu.VMEM((16, LANES), jnp.int32),
            pltpu.SMEM((16, LANES), jnp.int32),
            pltpu.SemaphoreType.DMA,
        ],
        compiler_params=pltpu.CompilerParams(vmem_limit_bytes=24 * 2**20),
        cost_estimate=pl.CostEstimate(flops=2 * 512 * 2 * depth * width, bytes_accessed=4 * 2**20, transcendentals=0),
    )(core.reshape(1), owners, got, right, right2)


def spread_marks(marks):
    values = marks.astype(jnp.bfloat16)
    count_r, count_c = values.shape
    return jnp.broadcast_to(
        values[:, None, :, None], (count_r, ATOM_BLOCK, count_c, ATOM_BLOCK)
    ).reshape(count_r * ATOM_BLOCK, count_c * ATOM_BLOCK)


def dense_product(core, left, right, right2, occupancy):
    depth = right.shape[0]
    kept = left * spread_marks(occupancy)
    halves = jnp.dot(row_order(), kept, preferred_element_type=jnp.float32).astype(jnp.bfloat16)
    sent = jnp.broadcast_to(halves.reshape(2, 1, HALF, depth), (2, 8, HALF, depth)).reshape(16, HALF, depth)
    panels = lax.all_to_all(sent, ("core", "zlo", "x"), 0, 0, tiled=True).reshape(2, 8 * HALF, depth)
    own = lax.dynamic_index_in_dim(panels, core, 0, keepdims=False)
    other = lax.dynamic_index_in_dim(panels, 1 - core, 0, keepdims=False)
    return jnp.dot(own, right, preferred_element_type=jnp.float32) + jnp.dot(
        other, right2, preferred_element_type=jnp.float32
    )


def reduce_dense(product):
    width = product.shape[-1]
    parts = (product * WIRE_SCALE).astype(WIRE).reshape(8, 32, 2, width).transpose(1, 0, 2, 3)
    got = lax.all_to_all(parts, ("zhi", "y"), 0, 0, tiled=True)
    return jnp.sum(got.astype(jnp.float32), axis=0) * (1.0 / WIRE_SCALE)


def update(slab, chosen, sums):
    picked = jnp.sum(jnp.where(chosen.reshape(chosen.shape + (1,) * (sums.ndim - 1)), sums[None], 0.0), axis=1)
    return 1.5 * slab.astype(jnp.float32) - 0.5 * picked.reshape(slab.shape)


def body(left, right, occupancy, owners, slab):
    core = lax.axis_index("core")
    panels = jnp.arange(8)

    right2 = lax.ppermute(right, "core", [(0, 1), (1, 0)])
    packed, owners = lax.optimization_barrier((pack(occupancy, left), owners))
    got = lax.all_to_all(packed, ("core", "zlo", "x"), 0, 0, tiled=True)

    owned = jnp.any(owners[:, None] == panels[None, :], axis=0)
    number = jnp.sum(owned)
    slot_of_step = jnp.sum(owned[None, :] & (panels[None, :] < owners[:, None]), axis=1)

    def reduced(slots):
        def branch():
            product = unpack_product(slots, core, owners, got, right, right2)
            parts = (product * WIRE_SCALE).astype(WIRE).reshape(32, slots, TILE, LANES)
            came = lax.all_to_all(parts, ("zhi", "y"), 0, 0, tiled=True)
            sums = jnp.sum(came.astype(jnp.float32), axis=0) * (1.0 / WIRE_SCALE)
            return update(slab, slot_of_step[:, None] == jnp.arange(slots)[None, :], sums)

        return branch

    which = sum((number > slots).astype(jnp.int32) for slots in DISTINCT[:-1])
    updated = lax.switch(which, [reduced(slots) for slots in DISTINCT])

    return lax.cond(
        jnp.isnan(updated[0, 0, 0]),
        lambda: update(slab, owners[:, None] == panels[None, :], reduce_dense(dense_product(core, left, right, right2, occupancy))),
        lambda: updated,
    )


def solution(mesh):
    fine = Mesh(mesh.devices.reshape(4, 8, 2, 2, 4), ("zhi", "y", "core", "zlo", "x"))
    row, col = ("zhi", "y", "core"), ("zlo", "x")
    in_specs = (P(col, row), P(row, col), P(col, row), P(), P(None, row, col))
    out_specs = P(None, row, col)
    return jax.shard_map(body, mesh=fine, in_specs=in_specs, out_specs=out_specs, check_vma=False)
```

```python
import functools

import jax
import jax.numpy as jnp
from jax import lax
from jax.experimental import pallas as pl
from jax.experimental.pallas import tpu as pltpu
from jax.sharding import Mesh, PartitionSpec as P

ATOM_BLOCK = 64
PANEL_ROWS = 128
HALF = 64
SLOTS = 8
LANES = 128
TILE = 8
DISTINCT = (3, 4, 5, 6, 7, 8)
PACKED_ROWS = SLOTS // 2 * 32
LIST_ROWS = 16
WIRE = jnp.float16
WIRE_SCALE = 128.0


def row_order():
    place = lax.broadcasted_iota(jnp.int32, (PANEL_ROWS, PANEL_ROWS), 0)
    row = lax.broadcasted_iota(jnp.int32, (PANEL_ROWS, PANEL_ROWS), 1)
    core, at, b = place // HALF, (place % HALF) // 2, place % 2
    return (row == at * 4 + core * 2 + b).astype(jnp.bfloat16)


def pack_kernel(marks_ref, left_ref, out_ref, rows, tiles):
    rows[...] = jnp.dot(row_order(), left_ref[...], preferred_element_type=jnp.float32).astype(jnp.bfloat16)
    tiles[...] = jnp.zeros_like(tiles)
    lane = lax.broadcasted_iota(jnp.int32, (32, LANES), 1)
    list_lane = lax.broadcasted_iota(jnp.int32, (LIST_ROWS, LANES), 1)
    block_rows, block_cols = marks_ref.shape
    count = jnp.int32(0)
    listed = jnp.zeros((LIST_ROWS, LANES), jnp.float32)
    for i in range(block_rows):
        for j in range(block_cols):
            kept = marks_ref[i, j] != 0
            slot = jnp.minimum(count, SLOTS - 1)
            fits = jnp.logical_and(kept, count < SLOTS)

            @pl.when(fits)
            def _(i=i, j=j, slot=slot):
                side = lax.rem(slot, 2)
                here = lane // ATOM_BLOCK == side
                at = pl.ds(pl.multiple_of(lax.div(slot, 2) * 32, 32), 32)
                for half in range(2):
                    block = rows[half * HALF + i * 32 : half * HALF + i * 32 + 32, j // 2 * LANES : (j // 2 + 1) * LANES]
                    turned = pltpu.roll(block, ATOM_BLOCK, 1)
                    placed = jnp.where(side == j % 2, block, turned)
                    tiles[half, at, :] = jnp.where(here, placed, tiles[half, at, :])

            mark = jnp.where(fits, 1.0, 0.0)
            listed = listed + jnp.where(list_lane == slot, mark * i, 0.0)
            listed = listed + jnp.where(list_lane == slot + 16, mark * j, 0.0)
            count = count + kept.astype(jnp.int32)
    listed = listed + jnp.where(list_lane == 32, count.astype(jnp.float32), 0.0)
    for to in range(out_ref.shape[0]):
        out_ref[to, :PACKED_ROWS, :] = tiles[to // 8]
        out_ref[to, PACKED_ROWS:, :] = listed.astype(jnp.bfloat16)


def destination_order(owners_ref, slots):
    place = lax.broadcasted_iota(jnp.int32, (32 * slots, 1), 0)
    at = sum((place >= k * 2 * slots).astype(jnp.int32) for k in range(1, 16))
    slot, b = (place - at * (2 * slots)) // 2, place % 2
    wanted = at * 2 + b
    filled = jnp.int32(0)
    for panel in range(8):
        owned = functools.reduce(jnp.logical_or, [owners_ref[t] == panel for t in range(owners_ref.shape[0])])
        wanted = wanted + jnp.where(slot == jnp.where(owned, filled, slots), panel * 32, 0)
        filled = filled + owned.astype(jnp.int32)
    row = lax.broadcasted_iota(jnp.int32, (32 * slots, 256), 1)
    return (row == wanted).astype(jnp.bfloat16)


def product_kernel(slots, core_ref, owners_ref, got_ref, right_ref, right2_ref, out_ref, flag_ref, dense, lists, places, sem):
    sources = got_ref.shape[0]
    depth = right_ref.shape[0]
    core = core_ref[0]
    for source in range(sources):
        lists[source : source + 1, :] = got_ref[source, PACKED_ROWS : PACKED_ROWS + 1, :].astype(jnp.int32)
    copy = pltpu.make_async_copy(lists, places, sem)
    copy.start()
    dense[...] = jnp.zeros_like(dense)
    order = destination_order(owners_ref, slots)
    copy.wait()
    side_of_lane = lax.broadcasted_iota(jnp.int32, (32, LANES), 1) // ATOM_BLOCK

    def put(source, first, slots_here):
        for slot in slots_here:
            i = places[source, slot]
            j = places[source, slot + 16]
            block = got_ref[source, slot // 2 * 32 : slot // 2 * 32 + 32, :]
            turned = pltpu.roll(block, ATOM_BLOCK, 1)
            side = lax.rem(j, 2)
            placed = jnp.where(side == slot % 2, block, turned)
            to_rows = pl.ds(pl.multiple_of(i * 256 + source % 8 * 32, 32), 32)
            to_lanes = pl.ds(pl.multiple_of(first + lax.div(j, 2) * LANES, LANES), LANES)
            here = side_of_lane == jnp.where(slot < places[source, 32], side, 2)
            dense[to_rows, to_lanes] = jnp.where(here, placed, dense[to_rows, to_lanes])

    firsts = [jnp.where(core == source // 8, 0, depth) for source in range(sources)]
    for source in range(sources):
        put(source, firsts[source], range(SLOTS // 2))
    most = jnp.int32(0)
    for source in range(sources):
        most = jnp.maximum(most, places[source, 32])

        @pl.when(places[source, 32] > SLOTS // 2)
        def _(source=source):
            put(source, firsts[source], range(SLOTS // 2, SLOTS))

    flag_ref[0] = (most > SLOTS).astype(jnp.int32)

    size = 32 * slots
    for i in range(2):
        rows = jnp.dot(order, dense[i * 256 : i * 256 + 256, :], preferred_element_type=jnp.float32).astype(jnp.bfloat16)
        sums = jnp.dot(rows[:, :depth], right_ref[...], preferred_element_type=jnp.float32) + jnp.dot(
            rows[:, depth:], right2_ref[...], preferred_element_type=jnp.float32
        )
        parts = sums.shape[1] // LANES
        for q in range(parts):
            out_ref[pl.ds(i * size * parts + q, size, stride=parts), :] = sums[:, q * LANES : (q + 1) * LANES]


def pack(marks, left):
    return pl.pallas_call(
        pack_kernel,
        out_shape=jax.ShapeDtypeStruct((16, PACKED_ROWS + LIST_ROWS, LANES), jnp.bfloat16),
        in_specs=[pl.BlockSpec(memory_space=pltpu.SMEM), pl.BlockSpec(memory_space=pltpu.VMEM)],
        out_specs=pl.BlockSpec(memory_space=pltpu.VMEM),
        scratch_shapes=[
            pltpu.VMEM(left.shape, jnp.bfloat16),
            pltpu.VMEM((2, PACKED_ROWS, LANES), jnp.bfloat16),
        ],
    )(marks, left)


def unpack_product(slots, core, owners, got, right, right2):
    depth, width = right.shape
    return pl.pallas_call(
        functools.partial(product_kernel, slots),
        out_shape=[
            jax.ShapeDtypeStruct((32 * slots * 2 * (width // LANES), LANES), jnp.float32),
            jax.ShapeDtypeStruct((1,), jnp.int32),
        ],
        in_specs=[pl.BlockSpec(memory_space=pltpu.SMEM)] * 2 + [pl.BlockSpec(memory_space=pltpu.VMEM)] * 3,
        out_specs=[pl.BlockSpec(memory_space=pltpu.VMEM), pl.BlockSpec(memory_space=pltpu.SMEM)],
        scratch_shapes=[
            pltpu.VMEM((512, 2 * depth), jnp.bfloat16),
            pltpu.VMEM((16, LANES), jnp.int32),
            pltpu.SMEM((16, LANES), jnp.int32),
            pltpu.SemaphoreType.DMA,
        ],
        compiler_params=pltpu.CompilerParams(vmem_limit_bytes=24 * 2**20),
        cost_estimate=pl.CostEstimate(flops=2 * 512 * 2 * depth * width, bytes_accessed=4 * 2**20, transcendentals=0),
    )(core.reshape(1), owners, got, right, right2)


def spread_marks(marks):
    values = marks.astype(jnp.bfloat16)
    count_r, count_c = values.shape
    return jnp.broadcast_to(
        values[:, None, :, None], (count_r, ATOM_BLOCK, count_c, ATOM_BLOCK)
    ).reshape(count_r * ATOM_BLOCK, count_c * ATOM_BLOCK)


def dense_product(slots, core, owners, left, right, right2, occupancy):
    depth, width = right.shape
    kept = left * spread_marks(occupancy)
    halves = jnp.dot(row_order(), kept, preferred_element_type=jnp.float32).astype(jnp.bfloat16)
    sent = jnp.broadcast_to(halves.reshape(2, 1, HALF, depth), (2, 8, HALF, depth)).reshape(16, HALF, depth)
    panels = lax.all_to_all(sent, ("core", "zlo", "x"), 0, 0, tiled=True).reshape(2, 8 * HALF, depth)
    own = lax.dynamic_index_in_dim(panels, core, 0, keepdims=False)
    other = lax.dynamic_index_in_dim(panels, 1 - core, 0, keepdims=False)
    product = jnp.dot(own, right, preferred_element_type=jnp.float32) + jnp.dot(
        other, right2, preferred_element_type=jnp.float32
    )
    number = jnp.arange(8)
    owned = jnp.any(owners[:, None] == number[None, :], axis=0)
    before = jnp.sum(owned[:, None] & (number[:, None] < number[None, :]), axis=0)
    panel_of_slot = jnp.sum(jnp.where(owned[None, :] & (before[None, :] == number[:slots, None]), number[None, :], 0), axis=1)
    chosen = jnp.take(product.reshape(8, 32, 2 * width // LANES, LANES), panel_of_slot, axis=0)
    return chosen.transpose(1, 0, 2, 3).reshape(-1, LANES)


def update(slab, chosen, sums):
    picked = jnp.sum(jnp.where(chosen.reshape(chosen.shape + (1,) * (sums.ndim - 1)), sums[None], 0.0), axis=1)
    return 1.5 * slab.astype(jnp.float32) - 0.5 * picked.reshape(slab.shape)


def body(left, right, occupancy, owners, slab):
    core = lax.axis_index("core")
    panels = jnp.arange(8)

    right2 = lax.ppermute(right, "core", [(0, 1), (1, 0)])
    packed, owners = lax.optimization_barrier((pack(occupancy, left), owners))
    got = lax.all_to_all(packed, ("core", "zlo", "x"), 0, 0, tiled=True)

    owned = jnp.any(owners[:, None] == panels[None, :], axis=0)
    number = jnp.sum(owned)
    slot_of_step = jnp.sum(owned[None, :] & (panels[None, :] < owners[:, None]), axis=1)

    def reduced(slots):
        def branch():
            product, flag = unpack_product(slots, core, owners, got, right, right2)
            product = lax.switch(
                flag[0],
                [lambda: product, lambda: dense_product(slots, core, owners, left, right, right2, occupancy)],
            )
            parts = (product * WIRE_SCALE).astype(WIRE).reshape(32, slots, TILE, LANES)
            came = lax.all_to_all(parts, ("zhi", "y"), 0, 0, tiled=True)
            sums = jnp.sum(came.astype(jnp.float32), axis=0) * (1.0 / WIRE_SCALE)
            return update(slab, slot_of_step[:, None] == jnp.arange(slots)[None, :], sums)

        return branch

    which = sum((number > slots).astype(jnp.int32) for slots in DISTINCT[:-1])
    return lax.switch(which, [reduced(slots) for slots in DISTINCT])


def solution(mesh):
    fine = Mesh(mesh.devices.reshape(4, 8, 2, 2, 4), ("zhi", "y", "core", "zlo", "x"))
    row, col = ("zhi", "y", "core"), ("zlo", "x")
    in_specs = (P(col, row), P(row, col), P(col, row), P(), P(None, row, col))
    out_specs = P(None, row, col)
    return jax.shard_map(body, mesh=fine, in_specs=in_specs, out_specs=out_specs, check_vma=False)
```

```python
import functools

import jax
import jax.numpy as jnp
from jax import lax
from jax.experimental import pallas as pl
from jax.experimental.pallas import tpu as pltpu
from jax.sharding import Mesh, PartitionSpec as P

ATOM_BLOCK = 64
PANEL_ROWS = 128
HALF = 64
SLOTS = 8
LANES = 128
TILE = 8
DISTINCT = (3, 4, 5, 6, 7, 8)
PACKED_ROWS = SLOTS // 2 * 32
LIST_ROWS = 16
WIRE = jnp.float16
WIRE_SCALE = 128.0


def row_order():
    place = lax.broadcasted_iota(jnp.int32, (PANEL_ROWS, PANEL_ROWS), 0)
    row = lax.broadcasted_iota(jnp.int32, (PANEL_ROWS, PANEL_ROWS), 1)
    core, at, b = place // HALF, (place % HALF) // 2, place % 2
    return (row == at * 4 + core * 2 + b).astype(jnp.bfloat16)


def pack_kernel(marks_ref, left_ref, out_ref, rows, tiles):
    rows[...] = jnp.dot(row_order(), left_ref[...], preferred_element_type=jnp.float32).astype(jnp.bfloat16)
    tiles[...] = jnp.zeros_like(tiles)
    lane = lax.broadcasted_iota(jnp.int32, (32, LANES), 1)
    list_lane = lax.broadcasted_iota(jnp.int32, (LIST_ROWS, LANES), 1)
    block_rows, block_cols = marks_ref.shape
    count = jnp.int32(0)
    listed = jnp.zeros((LIST_ROWS, LANES), jnp.float32)
    for i in range(block_rows):
        for j in range(block_cols):
            kept = marks_ref[i, j] != 0
            slot = jnp.minimum(count, SLOTS - 1)
            fits = jnp.logical_and(kept, count < SLOTS)

            @pl.when(fits)
            def _(i=i, j=j, slot=slot):
                side = lax.rem(slot, 2)
                here = lane // ATOM_BLOCK == side
                at = pl.ds(pl.multiple_of(lax.div(slot, 2) * 32, 32), 32)
                for half in range(2):
                    block = rows[half * HALF + i * 32 : half * HALF + i * 32 + 32, j // 2 * LANES : (j // 2 + 1) * LANES]
                    turned = pltpu.roll(block, ATOM_BLOCK, 1)
                    placed = jnp.where(side == j % 2, block, turned)
                    tiles[half, at, :] = jnp.where(here, placed, tiles[half, at, :])

            mark = jnp.where(fits, 1.0, 0.0)
            listed = listed + jnp.where(list_lane == slot, mark * i, 0.0)
            listed = listed + jnp.where(list_lane == slot + 16, mark * j, 0.0)
            count = count + kept.astype(jnp.int32)
    listed = listed + jnp.where(list_lane == 32, count.astype(jnp.float32), 0.0)
    for to in range(out_ref.shape[0]):
        out_ref[to, :PACKED_ROWS, :] = tiles[to // 8]
        out_ref[to, PACKED_ROWS:, :] = listed.astype(jnp.bfloat16)


def destination_order(owners_ref, slots):
    place = lax.broadcasted_iota(jnp.int32, (32 * slots, 1), 0)
    at = sum((place >= k * 2 * slots).astype(jnp.int32) for k in range(1, 16))
    slot, b = (place - at * (2 * slots)) // 2, place % 2
    wanted = at * 2 + b
    filled = jnp.int32(0)
    for panel in range(8):
        owned = functools.reduce(jnp.logical_or, [owners_ref[t] == panel for t in range(owners_ref.shape[0])])
        wanted = wanted + jnp.where(slot == jnp.where(owned, filled, slots), panel * 32, 0)
        filled = filled + owned.astype(jnp.int32)
    row = lax.broadcasted_iota(jnp.int32, (32 * slots, 256), 1)
    return (row == wanted).astype(jnp.bfloat16)


def product_kernel(slots, core_ref, owners_ref, got_ref, right_ref, right2_ref, out_ref, flag_ref, dense, ordered, lists, places, sem):
    sources = got_ref.shape[0]
    depth = right_ref.shape[0]
    core = core_ref[0]
    for source in range(sources):
        lists[source : source + 1, :] = got_ref[source, PACKED_ROWS : PACKED_ROWS + 1, :].astype(jnp.int32)
    copy = pltpu.make_async_copy(lists, places, sem)
    copy.start()
    dense[...] = jnp.zeros_like(dense)
    order = destination_order(owners_ref, slots)
    copy.wait()
    side_of_lane = lax.broadcasted_iota(jnp.int32, (32, LANES), 1) // ATOM_BLOCK

    def put(source, first, slots_here):
        for slot in slots_here:
            i = places[source, slot]
            j = places[source, slot + 16]
            block = got_ref[source, slot // 2 * 32 : slot // 2 * 32 + 32, :]
            turned = pltpu.roll(block, ATOM_BLOCK, 1)
            side = lax.rem(j, 2)
            placed = jnp.where(side == slot % 2, block, turned)
            to_rows = pl.ds(pl.multiple_of(i * 256 + source % 8 * 32, 32), 32)
            to_lanes = pl.ds(pl.multiple_of(first + lax.div(j, 2) * LANES, LANES), LANES)
            here = side_of_lane == jnp.where(slot < places[source, 32], side, 2)
            dense[to_rows, to_lanes] = jnp.where(here, placed, dense[to_rows, to_lanes])

    firsts = [jnp.where(core == source // 8, 0, depth) for source in range(sources)]
    for source in range(sources):
        put(source, firsts[source], range(SLOTS // 2))
    most = jnp.int32(0)
    for source in range(sources):
        most = jnp.maximum(most, places[source, 32])

        @pl.when(places[source, 32] > SLOTS // 2)
        def _(source=source):
            put(source, firsts[source], range(SLOTS // 2, SLOTS))

    flag_ref[0] = (most > SLOTS).astype(jnp.int32)

    size = 32 * slots
    for i in range(2):
        ordered[i * size : i * size + size, :] = jnp.dot(
            order, dense[i * 256 : i * 256 + 256, :], preferred_element_type=jnp.float32
        ).astype(jnp.bfloat16)
    sums = jnp.dot(ordered[:, :depth], right_ref[...], preferred_element_type=jnp.float32) + jnp.dot(
        ordered[:, depth:], right2_ref[...], preferred_element_type=jnp.float32
    )
    parts = sums.shape[1] // LANES
    for q in range(parts):
        out_ref[pl.ds(q, 2 * size, stride=parts), :] = sums[:, q * LANES : (q + 1) * LANES]


def pack(marks, left):
    return pl.pallas_call(
        pack_kernel,
        out_shape=jax.ShapeDtypeStruct((16, PACKED_ROWS + LIST_ROWS, LANES), jnp.bfloat16),
        in_specs=[pl.BlockSpec(memory_space=pltpu.SMEM), pl.BlockSpec(memory_space=pltpu.VMEM)],
        out_specs=pl.BlockSpec(memory_space=pltpu.VMEM),
        scratch_shapes=[
            pltpu.VMEM(left.shape, jnp.bfloat16),
            pltpu.VMEM((2, PACKED_ROWS, LANES), jnp.bfloat16),
        ],
    )(marks, left)


def unpack_product(slots, core, owners, got, right, right2):
    depth, width = right.shape
    return pl.pallas_call(
        functools.partial(product_kernel, slots),
        out_shape=[
            jax.ShapeDtypeStruct((32 * slots * 2 * (width // LANES), LANES), jnp.float32),
            jax.ShapeDtypeStruct((1,), jnp.int32),
        ],
        in_specs=[pl.BlockSpec(memory_space=pltpu.SMEM)] * 2 + [pl.BlockSpec(memory_space=pltpu.VMEM)] * 3,
        out_specs=[pl.BlockSpec(memory_space=pltpu.VMEM), pl.BlockSpec(memory_space=pltpu.SMEM)],
        scratch_shapes=[
            pltpu.VMEM((512, 2 * depth), jnp.bfloat16),
            pltpu.VMEM((64 * slots, 2 * depth), jnp.bfloat16),
            pltpu.VMEM((16, LANES), jnp.int32),
            pltpu.SMEM((16, LANES), jnp.int32),
            pltpu.SemaphoreType.DMA,
        ],
        compiler_params=pltpu.CompilerParams(vmem_limit_bytes=24 * 2**20),
        cost_estimate=pl.CostEstimate(flops=2 * 512 * 2 * depth * width, bytes_accessed=4 * 2**20, transcendentals=0),
    )(core.reshape(1), owners, got, right, right2)


def spread_marks(marks):
    values = marks.astype(jnp.bfloat16)
    count_r, count_c = values.shape
    return jnp.broadcast_to(
        values[:, None, :, None], (count_r, ATOM_BLOCK, count_c, ATOM_BLOCK)
    ).reshape(count_r * ATOM_BLOCK, count_c * ATOM_BLOCK)


def dense_product(slots, core, owners, left, right, right2, occupancy):
    depth, width = right.shape
    kept = left * spread_marks(occupancy)
    halves = jnp.dot(row_order(), kept, preferred_element_type=jnp.float32).astype(jnp.bfloat16)
    sent = jnp.broadcast_to(halves.reshape(2, 1, HALF, depth), (2, 8, HALF, depth)).reshape(16, HALF, depth)
    panels = lax.all_to_all(sent, ("core", "zlo", "x"), 0, 0, tiled=True).reshape(2, 8 * HALF, depth)
    own = lax.dynamic_index_in_dim(panels, core, 0, keepdims=False)
    other = lax.dynamic_index_in_dim(panels, 1 - core, 0, keepdims=False)
    product = jnp.dot(own, right, preferred_element_type=jnp.float32) + jnp.dot(
        other, right2, preferred_element_type=jnp.float32
    )
    number = jnp.arange(8)
    owned = jnp.any(owners[:, None] == number[None, :], axis=0)
    before = jnp.sum(owned[:, None] & (number[:, None] < number[None, :]), axis=0)
    panel_of_slot = jnp.sum(jnp.where(owned[None, :] & (before[None, :] == number[:slots, None]), number[None, :], 0), axis=1)
    chosen = jnp.take(product.reshape(8, 32, 2 * width // LANES, LANES), panel_of_slot, axis=0)
    return lax.optimization_barrier(chosen.transpose(1, 0, 2, 3).reshape(-1, LANES))


def update(slab, chosen, sums):
    picked = jnp.sum(jnp.where(chosen.reshape(chosen.shape + (1,) * (sums.ndim - 1)), sums[None], 0.0), axis=1)
    return 1.5 * slab.astype(jnp.float32) - 0.5 * picked.reshape(slab.shape)


def body(left, right, occupancy, owners, slab):
    core = lax.axis_index("core")
    panels = jnp.arange(8)

    right2 = lax.ppermute(right, "core", [(0, 1), (1, 0)])
    packed, owners = lax.optimization_barrier((pack(occupancy, left), owners))
    got = lax.all_to_all(packed, ("core", "zlo", "x"), 0, 0, tiled=True)

    owned = jnp.any(owners[:, None] == panels[None, :], axis=0)
    number = jnp.sum(owned)
    slot_of_step = jnp.sum(owned[None, :] & (panels[None, :] < owners[:, None]), axis=1)

    def reduced(slots):
        def branch():
            def to_wire(product):
                return (product * WIRE_SCALE).astype(WIRE).reshape(32, slots, TILE, LANES)

            product, flag = unpack_product(slots, core, owners, got, right, right2)
            parts = to_wire(product)
            parts = lax.switch(
                flag[0],
                [lambda: parts, lambda: to_wire(dense_product(slots, core, owners, left, right, right2, occupancy))],
            )
            came = lax.all_to_all(parts, ("zhi", "y"), 0, 0, tiled=True)
            sums = jnp.sum(came.astype(jnp.float32), axis=0) * (1.0 / WIRE_SCALE)
            return update(slab, slot_of_step[:, None] == jnp.arange(slots)[None, :], sums)

        return branch

    which = sum((number > slots).astype(jnp.int32) for slots in DISTINCT[:-1])
    return lax.switch(which, [reduced(slots) for slots in DISTINCT])


def solution(mesh):
    fine = Mesh(mesh.devices.reshape(4, 8, 2, 2, 4), ("zhi", "y", "core", "zlo", "x"))
    row, col = ("zhi", "y", "core"), ("zlo", "x")
    in_specs = (P(col, row), P(row, col), P(col, row), P(), P(None, row, col))
    out_specs = P(None, row, col)
    return jax.shard_map(body, mesh=fine, in_specs=in_specs, out_specs=out_specs, check_vma=False)
```

```python
import functools

import jax
import jax.numpy as jnp
from jax import lax
from jax.experimental import pallas as pl
from jax.experimental.pallas import tpu as pltpu
from jax.sharding import Mesh, PartitionSpec as P

ATOM_BLOCK = 64
PANEL_ROWS = 128
HALF = 64
SLOTS = 8
LANES = 128
TILE = 8
DISTINCT = (3, 4, 5, 6, 7, 8)
LAST = 4
MEMBERS = [(member - LAST) % 32 for member in range(32)]
PACKED_ROWS = SLOTS // 2 * 32
LIST_ROWS = 16
WIRE = jnp.float16
WIRE_SCALE = 128.0


def row_order():
    place = lax.broadcasted_iota(jnp.int32, (PANEL_ROWS, PANEL_ROWS), 0)
    row = lax.broadcasted_iota(jnp.int32, (PANEL_ROWS, PANEL_ROWS), 1)
    core, at, b = place // HALF, (place % HALF) // 2, place % 2
    return (row == at * 4 + core * 2 + b).astype(jnp.bfloat16)


def pack_kernel(marks_ref, left_ref, out_ref, rows, tiles):
    rows[...] = jnp.dot(row_order(), left_ref[...], preferred_element_type=jnp.float32).astype(jnp.bfloat16)
    tiles[...] = jnp.zeros_like(tiles)
    lane = lax.broadcasted_iota(jnp.int32, (32, LANES), 1)
    list_lane = lax.broadcasted_iota(jnp.int32, (LIST_ROWS, LANES), 1)
    block_rows, block_cols = marks_ref.shape
    count = jnp.int32(0)
    listed = jnp.zeros((LIST_ROWS, LANES), jnp.float32)
    for i in range(block_rows):
        for j in range(block_cols):
            kept = marks_ref[i, j] != 0
            slot = jnp.minimum(count, SLOTS - 1)
            fits = jnp.logical_and(kept, count < SLOTS)

            @pl.when(fits)
            def _(i=i, j=j, slot=slot):
                side = lax.rem(slot, 2)
                here = lane // ATOM_BLOCK == side
                at = pl.ds(pl.multiple_of(lax.div(slot, 2) * 32, 32), 32)
                for half in range(2):
                    block = rows[half * HALF + i * 32 : half * HALF + i * 32 + 32, j // 2 * LANES : (j // 2 + 1) * LANES]
                    turned = pltpu.roll(block, ATOM_BLOCK, 1)
                    placed = jnp.where(side == j % 2, block, turned)
                    tiles[half, at, :] = jnp.where(here, placed, tiles[half, at, :])

            mark = jnp.where(fits, 1.0, 0.0)
            listed = listed + jnp.where(list_lane == slot, mark * i, 0.0)
            listed = listed + jnp.where(list_lane == slot + 16, mark * j, 0.0)
            count = count + kept.astype(jnp.int32)
    listed = listed + jnp.where(list_lane == 32, count.astype(jnp.float32), 0.0)
    for to in range(out_ref.shape[0]):
        out_ref[to, :PACKED_ROWS, :] = tiles[to // 8]
        out_ref[to, PACKED_ROWS:, :] = listed.astype(jnp.bfloat16)


def destination_order(places, row_of_owners, slots):
    place = lax.broadcasted_iota(jnp.int32, (32 * slots, 1), 0)
    at = sum((place >= k * 2 * slots).astype(jnp.int32) for k in range(1, 16))
    slot, b = (place - at * (2 * slots)) // 2, place % 2
    wanted = at * 2 + b
    filled = jnp.int32(0)
    owners = [places[row_of_owners, t] for t in range(8)]
    for panel in range(8):
        owned = functools.reduce(jnp.logical_or, [owner == panel for owner in owners])
        wanted = wanted + jnp.where(slot == jnp.where(owned, filled, slots), panel * 32, 0)
        filled = filled + owned.astype(jnp.int32)
    row = lax.broadcasted_iota(jnp.int32, (32 * slots, 256), 1)
    return (row == wanted).astype(jnp.bfloat16)


def product_kernel(slots, facts_ref, got_ref, right_ref, right2_ref, out_ref, flag_ref, dense, ordered, lists, places, sem):
    sources = got_ref.shape[0]
    depth = right_ref.shape[0]
    lists[sources : sources + 1, :] = facts_ref[...]
    for source in range(sources):
        lists[source : source + 1, :] = got_ref[source, PACKED_ROWS : PACKED_ROWS + 1, :].astype(jnp.int32)
    copy = pltpu.make_async_copy(lists, places, sem)
    copy.start()
    dense[...] = jnp.zeros_like(dense)
    copy.wait()
    core = places[sources, 8]
    order = destination_order(places, sources, slots)
    side_of_lane = lax.broadcasted_iota(jnp.int32, (32, LANES), 1) // ATOM_BLOCK

    def put(source, first, slots_here):
        for slot in slots_here:
            i = places[source, slot]
            j = places[source, slot + 16]
            block = got_ref[source, slot // 2 * 32 : slot // 2 * 32 + 32, :]
            turned = pltpu.roll(block, ATOM_BLOCK, 1)
            side = lax.rem(j, 2)
            placed = jnp.where(side == slot % 2, block, turned)
            to_rows = pl.ds(pl.multiple_of(i * 256 + source % 8 * 32, 32), 32)
            to_lanes = pl.ds(pl.multiple_of(first + lax.div(j, 2) * LANES, LANES), LANES)
            here = side_of_lane == jnp.where(slot < places[source, 32], side, 2)
            dense[to_rows, to_lanes] = jnp.where(here, placed, dense[to_rows, to_lanes])

    firsts = [jnp.where(core == source // 8, 0, depth) for source in range(sources)]
    for source in range(sources):
        put(source, firsts[source], range(SLOTS // 2))
    most = jnp.int32(0)
    for source in range(sources):
        most = jnp.maximum(most, places[source, 32])

        @pl.when(places[source, 32] > SLOTS // 2)
        def _(source=source):
            put(source, firsts[source], range(SLOTS // 2, SLOTS))

    flag_ref[0] = (most > SLOTS).astype(jnp.int32)

    size = 32 * slots
    for i in range(2):
        ordered[i * size : i * size + size, :] = jnp.dot(
            order, dense[i * 256 : i * 256 + 256, :], preferred_element_type=jnp.float32
        ).astype(jnp.bfloat16)
    sums = jnp.dot(ordered[:, :depth], right_ref[...], preferred_element_type=jnp.float32) + jnp.dot(
        ordered[:, depth:], right2_ref[...], preferred_element_type=jnp.float32
    )
    parts = sums.shape[1] // LANES
    first = LAST * 2 * slots
    for q in range(parts):
        columns = sums[:, q * LANES : (q + 1) * LANES]
        out_ref[pl.ds(q, first, stride=parts), :] = columns[2 * size - first :]
        out_ref[pl.ds(first * parts + q, 2 * size - first, stride=parts), :] = columns[: 2 * size - first]


def pack(marks, left):
    return pl.pallas_call(
        pack_kernel,
        out_shape=jax.ShapeDtypeStruct((16, PACKED_ROWS + LIST_ROWS, LANES), jnp.bfloat16),
        in_specs=[pl.BlockSpec(memory_space=pltpu.SMEM), pl.BlockSpec(memory_space=pltpu.VMEM)],
        out_specs=pl.BlockSpec(memory_space=pltpu.VMEM),
        scratch_shapes=[
            pltpu.VMEM(left.shape, jnp.bfloat16),
            pltpu.VMEM((2, PACKED_ROWS, LANES), jnp.bfloat16),
        ],
    )(marks, left)


def unpack_product(slots, facts, got, right, right2):
    depth, width = right.shape
    return pl.pallas_call(
        functools.partial(product_kernel, slots),
        out_shape=[
            jax.ShapeDtypeStruct((32 * slots * 2 * (width // LANES), LANES), jnp.float32),
            jax.ShapeDtypeStruct((1,), jnp.int32),
        ],
        in_specs=[pl.BlockSpec(memory_space=pltpu.VMEM)] * 4,
        out_specs=[pl.BlockSpec(memory_space=pltpu.VMEM), pl.BlockSpec(memory_space=pltpu.SMEM)],
        scratch_shapes=[
            pltpu.VMEM((512, 2 * depth), jnp.bfloat16),
            pltpu.VMEM((64 * slots, 2 * depth), jnp.bfloat16),
            pltpu.VMEM((24, LANES), jnp.int32),
            pltpu.SMEM((24, LANES), jnp.int32),
            pltpu.SemaphoreType.DMA,
        ],
        compiler_params=pltpu.CompilerParams(vmem_limit_bytes=24 * 2**20),
        cost_estimate=pl.CostEstimate(flops=2 * 512 * 2 * depth * width, bytes_accessed=4 * 2**20, transcendentals=0),
    )(facts, got, right, right2)


def spread_marks(marks):
    values = marks.astype(jnp.bfloat16)
    count_r, count_c = values.shape
    return jnp.broadcast_to(
        values[:, None, :, None], (count_r, ATOM_BLOCK, count_c, ATOM_BLOCK)
    ).reshape(count_r * ATOM_BLOCK, count_c * ATOM_BLOCK)


def dense_product(slots, core, owners, left, right, right2, occupancy):
    depth, width = right.shape
    kept = left * spread_marks(occupancy)
    halves = jnp.dot(row_order(), kept, preferred_element_type=jnp.float32).astype(jnp.bfloat16)
    sent = jnp.broadcast_to(halves.reshape(2, 1, HALF, depth), (2, 8, HALF, depth)).reshape(16, HALF, depth)
    panels = lax.all_to_all(sent, ("core", "zlo", "x"), 0, 0, tiled=True).reshape(2, 8 * HALF, depth)
    own = lax.dynamic_index_in_dim(panels, core, 0, keepdims=False)
    other = lax.dynamic_index_in_dim(panels, 1 - core, 0, keepdims=False)
    product = jnp.dot(own, right, preferred_element_type=jnp.float32) + jnp.dot(
        other, right2, preferred_element_type=jnp.float32
    )
    number = jnp.arange(8)
    owned = jnp.any(owners[:, None] == number[None, :], axis=0)
    before = jnp.sum(owned[:, None] & (number[:, None] < number[None, :]), axis=0)
    panel_of_slot = jnp.sum(jnp.where(owned[None, :] & (before[None, :] == number[:slots, None]), number[None, :], 0), axis=1)
    chosen = jnp.take(product.reshape(8, 32, 2 * width // LANES, LANES), panel_of_slot, axis=0)
    return lax.optimization_barrier(jnp.roll(chosen.transpose(1, 0, 2, 3), LAST, axis=0).reshape(-1, LANES))


def update(slab, chosen, sums):
    picked = jnp.sum(jnp.where(chosen.reshape(chosen.shape + (1,) * (sums.ndim - 1)), sums[None], 0.0), axis=1)
    return 1.5 * slab.astype(jnp.float32) - 0.5 * picked.reshape(slab.shape)


def body(left, right, occupancy, owners, slab):
    core = lax.axis_index("core")
    panels = jnp.arange(8)

    right2 = lax.ppermute(right, "core", [(0, 1), (1, 0)])
    packed, owners = lax.optimization_barrier((pack(occupancy, left), owners))
    got = lax.all_to_all(packed, ("core", "zlo", "x"), 0, 0, tiled=True)

    owned = jnp.any(owners[:, None] == panels[None, :], axis=0)
    number = jnp.sum(owned)
    slot_of_step = jnp.sum(owned[None, :] & (panels[None, :] < owners[:, None]), axis=1)

    facts = jnp.pad(jnp.concatenate([owners, core.reshape(1)]), (0, LANES - 9)).reshape(1, LANES)

    def reduced(slots):
        def branch():
            def to_wire(product):
                return (product * WIRE_SCALE).astype(WIRE).reshape(32, slots, TILE, LANES)

            product, flag = unpack_product(slots, facts, got, right, right2)
            parts = to_wire(product)
            parts = lax.switch(
                flag[0],
                [lambda: parts, lambda: to_wire(dense_product(slots, core, owners, left, right, right2, occupancy))],
            )
            came = lax.all_to_all(parts, ("zhi", "y"), 0, 0, axis_index_groups=[MEMBERS], tiled=True)
            sums = jnp.sum(came.astype(jnp.float32), axis=0) * (1.0 / WIRE_SCALE)
            return update(slab, slot_of_step[:, None] == jnp.arange(slots)[None, :], sums)

        return branch

    which = sum((number > slots).astype(jnp.int32) for slots in DISTINCT[:-1])
    return lax.switch(which, [reduced(slots) for slots in DISTINCT])


def solution(mesh):
    fine = Mesh(mesh.devices.reshape(4, 8, 2, 2, 4), ("zhi", "y", "core", "zlo", "x"))
    row, col = ("zhi", "y", "core"), ("zlo", "x")
    in_specs = (P(col, row), P(row, col), P(col, row), P(), P(None, row, col))
    out_specs = P(None, row, col)
    return jax.shard_map(body, mesh=fine, in_specs=in_specs, out_specs=out_specs, check_vma=False)
```

```python
import functools

import jax
import jax.numpy as jnp
from jax import lax
from jax.experimental import pallas as pl
from jax.experimental.pallas import tpu as pltpu
from jax.sharding import Mesh, PartitionSpec as P

ATOM_BLOCK = 64
PANEL_ROWS = 128
HALF = 64
SLOTS = 8
LANES = 128
TILE = 8
DISTINCT = (3, 4, 5, 6, 7, 8)
MEMBERS = [(3 + j) % 4 * 8 + (4 + j // 4 * 3) % 8 for j in range(32)]
PACKED_ROWS = SLOTS // 2 * 32
LIST_ROWS = 16
WIRE = jnp.float16
WIRE_SCALE = 128.0


def row_order():
    place = lax.broadcasted_iota(jnp.int32, (PANEL_ROWS, PANEL_ROWS), 0)
    row = lax.broadcasted_iota(jnp.int32, (PANEL_ROWS, PANEL_ROWS), 1)
    core, at, b = place // HALF, (place % HALF) // 2, place % 2
    return (row == at * 4 + core * 2 + b).astype(jnp.bfloat16)


def pack_kernel(marks_ref, left_ref, out_ref, rows, tiles):
    rows[...] = jnp.dot(row_order(), left_ref[...], preferred_element_type=jnp.float32).astype(jnp.bfloat16)
    tiles[...] = jnp.zeros_like(tiles)
    lane = lax.broadcasted_iota(jnp.int32, (32, LANES), 1)
    list_lane = lax.broadcasted_iota(jnp.int32, (LIST_ROWS, LANES), 1)
    block_rows, block_cols = marks_ref.shape
    count = jnp.int32(0)
    listed = jnp.zeros((LIST_ROWS, LANES), jnp.float32)
    for i in range(block_rows):
        for j in range(block_cols):
            kept = marks_ref[i, j] != 0
            slot = jnp.minimum(count, SLOTS - 1)
            fits = jnp.logical_and(kept, count < SLOTS)

            @pl.when(fits)
            def _(i=i, j=j, slot=slot):
                side = lax.rem(slot, 2)
                here = lane // ATOM_BLOCK == side
                at = pl.ds(pl.multiple_of(lax.div(slot, 2) * 32, 32), 32)
                for half in range(2):
                    block = rows[half * HALF + i * 32 : half * HALF + i * 32 + 32, j // 2 * LANES : (j // 2 + 1) * LANES]
                    turned = pltpu.roll(block, ATOM_BLOCK, 1)
                    placed = jnp.where(side == j % 2, block, turned)
                    tiles[half, at, :] = jnp.where(here, placed, tiles[half, at, :])

            mark = jnp.where(fits, 1.0, 0.0)
            listed = listed + jnp.where(list_lane == slot, mark * i, 0.0)
            listed = listed + jnp.where(list_lane == slot + 16, mark * j, 0.0)
            count = count + kept.astype(jnp.int32)
    listed = listed + jnp.where(list_lane == 32, count.astype(jnp.float32), 0.0)
    for to in range(out_ref.shape[0]):
        out_ref[to, :PACKED_ROWS, :] = tiles[to // 8]
        out_ref[to, PACKED_ROWS:, :] = listed.astype(jnp.bfloat16)


def destination_order(places, row_of_owners, slots):
    place = lax.broadcasted_iota(jnp.int32, (64 * slots, 1), 0)
    member = ((place.astype(jnp.float32) + 0.5) * (0.5 / slots)).astype(jnp.int32)
    rest = place - member * (2 * slots)
    slot, b = rest // 2, rest % 2
    zhi, y = (3 + member) % 4, (4 + member // 4 * 3) % 8
    wanted = zhi // 2 * 256 + zhi % 2 * 16 + y * 2 + b
    filled = jnp.int32(0)
    owners = [places[row_of_owners, t] for t in range(8)]
    for panel in range(8):
        owned = functools.reduce(jnp.logical_or, [owner == panel for owner in owners])
        wanted = wanted + jnp.where(slot == jnp.where(owned, filled, slots), panel * 32, 0)
        filled = filled + owned.astype(jnp.int32)
    row = lax.broadcasted_iota(jnp.int32, (64 * slots, 512), 1)
    return (row == wanted).astype(jnp.bfloat16)


def product_kernel(slots, facts_ref, got_ref, right_ref, right2_ref, out_ref, flag_ref, dense, ordered, lists, places, sem):
    sources = got_ref.shape[0]
    depth = right_ref.shape[0]
    lists[sources : sources + 1, :] = facts_ref[...]
    for source in range(sources):
        lists[source : source + 1, :] = got_ref[source, PACKED_ROWS : PACKED_ROWS + 1, :].astype(jnp.int32)
    copy = pltpu.make_async_copy(lists, places, sem)
    copy.start()
    dense[...] = jnp.zeros_like(dense)
    copy.wait()
    core = places[sources, 8]
    order = destination_order(places, sources, slots)
    side_of_lane = lax.broadcasted_iota(jnp.int32, (32, LANES), 1) // ATOM_BLOCK

    def put(source, first, slots_here):
        for slot in slots_here:
            i = places[source, slot]
            j = places[source, slot + 16]
            block = got_ref[source, slot // 2 * 32 : slot // 2 * 32 + 32, :]
            turned = pltpu.roll(block, ATOM_BLOCK, 1)
            side = lax.rem(j, 2)
            placed = jnp.where(side == slot % 2, block, turned)
            to_rows = pl.ds(pl.multiple_of(i * 256 + source % 8 * 32, 32), 32)
            to_lanes = pl.ds(pl.multiple_of(first + lax.div(j, 2) * LANES, LANES), LANES)
            here = side_of_lane == jnp.where(slot < places[source, 32], side, 2)
            dense[to_rows, to_lanes] = jnp.where(here, placed, dense[to_rows, to_lanes])

    firsts = [jnp.where(core == source // 8, 0, depth) for source in range(sources)]
    for source in range(sources):
        put(source, firsts[source], range(SLOTS // 2))
    most = jnp.int32(0)
    for source in range(sources):
        most = jnp.maximum(most, places[source, 32])

        @pl.when(places[source, 32] > SLOTS // 2)
        def _(source=source):
            put(source, firsts[source], range(SLOTS // 2, SLOTS))

    flag_ref[0] = (most > SLOTS).astype(jnp.int32)

    ordered[...] = jnp.dot(order, dense[...], preferred_element_type=jnp.float32).astype(jnp.bfloat16)
    sums = jnp.dot(ordered[:, :depth], right_ref[...], preferred_element_type=jnp.float32) + jnp.dot(
        ordered[:, depth:], right2_ref[...], preferred_element_type=jnp.float32
    )
    parts = sums.shape[1] // LANES
    for q in range(parts):
        out_ref[pl.ds(q, 64 * slots, stride=parts), :] = sums[:, q * LANES : (q + 1) * LANES]


def pack(marks, left):
    return pl.pallas_call(
        pack_kernel,
        out_shape=jax.ShapeDtypeStruct((16, PACKED_ROWS + LIST_ROWS, LANES), jnp.bfloat16),
        in_specs=[pl.BlockSpec(memory_space=pltpu.SMEM), pl.BlockSpec(memory_space=pltpu.VMEM)],
        out_specs=pl.BlockSpec(memory_space=pltpu.VMEM),
        scratch_shapes=[
            pltpu.VMEM(left.shape, jnp.bfloat16),
            pltpu.VMEM((2, PACKED_ROWS, LANES), jnp.bfloat16),
        ],
    )(marks, left)


def unpack_product(slots, facts, got, right, right2):
    depth, width = right.shape
    return pl.pallas_call(
        functools.partial(product_kernel, slots),
        out_shape=[
            jax.ShapeDtypeStruct((32 * slots * 2 * (width // LANES), LANES), jnp.float32),
            jax.ShapeDtypeStruct((1,), jnp.int32),
        ],
        in_specs=[pl.BlockSpec(memory_space=pltpu.VMEM)] * 4,
        out_specs=[pl.BlockSpec(memory_space=pltpu.VMEM), pl.BlockSpec(memory_space=pltpu.SMEM)],
        scratch_shapes=[
            pltpu.VMEM((512, 2 * depth), jnp.bfloat16),
            pltpu.VMEM((64 * slots, 2 * depth), jnp.bfloat16),
            pltpu.VMEM((24, LANES), jnp.int32),
            pltpu.SMEM((24, LANES), jnp.int32),
            pltpu.SemaphoreType.DMA,
        ],
        compiler_params=pltpu.CompilerParams(vmem_limit_bytes=24 * 2**20),
        cost_estimate=pl.CostEstimate(flops=2 * 512 * 2 * depth * width, bytes_accessed=4 * 2**20, transcendentals=0),
    )(facts, got, right, right2)


def spread_marks(marks):
    values = marks.astype(jnp.bfloat16)
    count_r, count_c = values.shape
    return jnp.broadcast_to(
        values[:, None, :, None], (count_r, ATOM_BLOCK, count_c, ATOM_BLOCK)
    ).reshape(count_r * ATOM_BLOCK, count_c * ATOM_BLOCK)


def dense_product(slots, core, owners, left, right, right2, occupancy):
    depth, width = right.shape
    kept = left * spread_marks(occupancy)
    halves = jnp.dot(row_order(), kept, preferred_element_type=jnp.float32).astype(jnp.bfloat16)
    sent = jnp.broadcast_to(halves.reshape(2, 1, HALF, depth), (2, 8, HALF, depth)).reshape(16, HALF, depth)
    panels = lax.all_to_all(sent, ("core", "zlo", "x"), 0, 0, tiled=True).reshape(2, 8 * HALF, depth)
    own = lax.dynamic_index_in_dim(panels, core, 0, keepdims=False)
    other = lax.dynamic_index_in_dim(panels, 1 - core, 0, keepdims=False)
    product = jnp.dot(own, right, preferred_element_type=jnp.float32) + jnp.dot(
        other, right2, preferred_element_type=jnp.float32
    )
    number = jnp.arange(8)
    owned = jnp.any(owners[:, None] == number[None, :], axis=0)
    before = jnp.sum(owned[:, None] & (number[:, None] < number[None, :]), axis=0)
    panel_of_slot = jnp.sum(jnp.where(owned[None, :] & (before[None, :] == number[:slots, None]), number[None, :], 0), axis=1)
    chosen = jnp.take(product.reshape(8, 32, 2 * width // LANES, LANES), panel_of_slot, axis=0)
    return lax.optimization_barrier(jnp.stack([chosen[:, member] for member in MEMBERS]).reshape(-1, LANES))


def update(slab, chosen, sums):
    picked = jnp.sum(jnp.where(chosen.reshape(chosen.shape + (1,) * (sums.ndim - 1)), sums[None], 0.0), axis=1)
    return 1.5 * slab.astype(jnp.float32) - 0.5 * picked.reshape(slab.shape)


def body(left, right, occupancy, owners, slab):
    core = lax.axis_index("core")
    panels = jnp.arange(8)

    right2 = lax.ppermute(right, "core", [(0, 1), (1, 0)])
    packed, owners = lax.optimization_barrier((pack(occupancy, left), owners))
    got = lax.all_to_all(packed, ("core", "zlo", "x"), 0, 0, tiled=True)

    owned = jnp.any(owners[:, None] == panels[None, :], axis=0)
    number = jnp.sum(owned)
    slot_of_step = jnp.sum(owned[None, :] & (panels[None, :] < owners[:, None]), axis=1)

    facts = jnp.pad(jnp.concatenate([owners, core.reshape(1)]), (0, LANES - 9)).reshape(1, LANES)

    def reduced(slots):
        def branch():
            def to_wire(product):
                return (product * WIRE_SCALE).astype(WIRE).reshape(32, slots, TILE, LANES)

            product, flag = unpack_product(slots, facts, got, right, right2)
            parts = to_wire(product)
            parts = lax.switch(
                flag[0],
                [lambda: parts, lambda: to_wire(dense_product(slots, core, owners, left, right, right2, occupancy))],
            )
            came = lax.all_to_all(parts, ("zhi", "y"), 0, 0, axis_index_groups=[MEMBERS], tiled=True)
            sums = jnp.sum(came.astype(jnp.float32), axis=0) * (1.0 / WIRE_SCALE)
            return update(slab, slot_of_step[:, None] == jnp.arange(slots)[None, :], sums)

        return branch

    which = sum((number > slots).astype(jnp.int32) for slots in DISTINCT[:-1])
    return lax.switch(which, [reduced(slots) for slots in DISTINCT])


def solution(mesh):
    fine = Mesh(mesh.devices.reshape(4, 8, 2, 2, 4), ("zhi", "y", "core", "zlo", "x"))
    row, col = ("zhi", "y", "core"), ("zlo", "x")
    in_specs = (P(col, row), P(row, col), P(col, row), P(), P(None, row, col))
    out_specs = P(None, row, col)
    return jax.shard_map(body, mesh=fine, in_specs=in_specs, out_specs=out_specs, check_vma=False)
```

```python
import functools

import jax
import jax.numpy as jnp
from jax import lax
from jax.experimental import pallas as pl
from jax.experimental.pallas import tpu as pltpu
from jax.sharding import Mesh, PartitionSpec as P

ATOM_BLOCK = 64
PANEL_ROWS = 128
HALF = 64
SLOTS = 8
LANES = 128
TILE = 8
DISTINCT = (4, 5, 6, 8)
LAST = 4
MEMBERS = [(member - LAST) % 32 for member in range(32)]
PACKED_ROWS = SLOTS // 2 * 32
LIST_ROWS = 16
WIRE = jnp.float16
WIRE_SCALE = 128.0


def row_order():
    place = lax.broadcasted_iota(jnp.int32, (PANEL_ROWS, PANEL_ROWS), 0)
    row = lax.broadcasted_iota(jnp.int32, (PANEL_ROWS, PANEL_ROWS), 1)
    core, at, b = place // HALF, (place % HALF) // 2, place % 2
    return (row == at * 4 + core * 2 + b).astype(jnp.bfloat16)


def pack_kernel(marks_ref, left_ref, out_ref, rows, tiles):
    rows[...] = jnp.dot(row_order(), left_ref[...], preferred_element_type=jnp.float32).astype(jnp.bfloat16)
    tiles[...] = jnp.zeros_like(tiles)
    lane = lax.broadcasted_iota(jnp.int32, (32, LANES), 1)
    list_lane = lax.broadcasted_iota(jnp.int32, (LIST_ROWS, LANES), 1)
    block_rows, block_cols = marks_ref.shape
    count = jnp.int32(0)
    listed = jnp.zeros((LIST_ROWS, LANES), jnp.float32)
    for i in range(block_rows):
        for j in range(block_cols):
            kept = marks_ref[i, j] != 0
            slot = jnp.minimum(count, SLOTS - 1)
            fits = jnp.logical_and(kept, count < SLOTS)

            @pl.when(fits)
            def _(i=i, j=j, slot=slot):
                side = lax.rem(slot, 2)
                here = lane // ATOM_BLOCK == side
                at = pl.ds(pl.multiple_of(lax.div(slot, 2) * 32, 32), 32)
                for half in range(2):
                    block = rows[half * HALF + i * 32 : half * HALF + i * 32 + 32, j // 2 * LANES : (j // 2 + 1) * LANES]
                    turned = pltpu.roll(block, ATOM_BLOCK, 1)
                    placed = jnp.where(side == j % 2, block, turned)
                    tiles[half, at, :] = jnp.where(here, placed, tiles[half, at, :])

            mark = jnp.where(fits, 1.0, 0.0)
            listed = listed + jnp.where(list_lane == slot, mark * i, 0.0)
            listed = listed + jnp.where(list_lane == slot + 16, mark * j, 0.0)
            count = count + kept.astype(jnp.int32)
    listed = listed + jnp.where(list_lane == 32, count.astype(jnp.float32), 0.0)
    for to in range(out_ref.shape[0]):
        out_ref[to, :PACKED_ROWS, :] = tiles[to // 8]
        out_ref[to, PACKED_ROWS:, :] = listed.astype(jnp.bfloat16)


def destination_order(places, row_of_owners, slots):
    place = lax.broadcasted_iota(jnp.int32, (32 * slots, 1), 0)
    at = sum((place >= k * 2 * slots).astype(jnp.int32) for k in range(1, 16))
    slot, b = (place - at * (2 * slots)) // 2, place % 2
    wanted = at * 2 + b
    filled = jnp.int32(0)
    owners = [places[row_of_owners, t] for t in range(8)]
    for panel in range(8):
        owned = functools.reduce(jnp.logical_or, [owner == panel for owner in owners])
        wanted = wanted + jnp.where(slot == jnp.where(owned, filled, slots), panel * 32, 0)
        filled = filled + owned.astype(jnp.int32)
    row = lax.broadcasted_iota(jnp.int32, (32 * slots, 256), 1)
    return (row == wanted).astype(jnp.bfloat16)


def product_kernel(slots, facts_ref, got_ref, right_ref, right2_ref, out_ref, flag_ref, dense, ordered, lists, places, sem):
    sources = got_ref.shape[0]
    depth = right_ref.shape[0]
    lists[sources : sources + 1, :] = facts_ref[...]
    for source in range(sources):
        lists[source : source + 1, :] = got_ref[source, PACKED_ROWS : PACKED_ROWS + 1, :].astype(jnp.int32)
    copy = pltpu.make_async_copy(lists, places, sem)
    copy.start()
    dense[...] = jnp.zeros_like(dense)
    copy.wait()
    core = places[sources, 8]
    order = destination_order(places, sources, slots)
    side_of_lane = lax.broadcasted_iota(jnp.int32, (32, LANES), 1) // ATOM_BLOCK

    def put(source, first, slots_here):
        for slot in slots_here:
            i = places[source, slot]
            j = places[source, slot + 16]
            block = got_ref[source, slot // 2 * 32 : slot // 2 * 32 + 32, :]
            turned = pltpu.roll(block, ATOM_BLOCK, 1)
            side = lax.rem(j, 2)
            placed = jnp.where(side == slot % 2, block, turned)
            to_rows = pl.ds(pl.multiple_of(i * 256 + source % 8 * 32, 32), 32)
            to_lanes = pl.ds(pl.multiple_of(first + lax.div(j, 2) * LANES, LANES), LANES)
            here = side_of_lane == jnp.where(slot < places[source, 32], side, 2)
            dense[to_rows, to_lanes] = jnp.where(here, placed, dense[to_rows, to_lanes])

    firsts = [jnp.where(core == source // 8, 0, depth) for source in range(sources)]
    for source in range(sources):
        put(source, firsts[source], range(SLOTS // 2))
    most = jnp.int32(0)
    for source in range(sources):
        most = jnp.maximum(most, places[source, 32])

        @pl.when(places[source, 32] > SLOTS // 2)
        def _(source=source):
            put(source, firsts[source], range(SLOTS // 2, SLOTS))

    flag_ref[0] = (most > SLOTS).astype(jnp.int32)

    size = 32 * slots
    for i in range(2):
        ordered[i * size : i * size + size, :] = jnp.dot(
            order, dense[i * 256 : i * 256 + 256, :], preferred_element_type=jnp.float32
        ).astype(jnp.bfloat16)
    sums = jnp.dot(ordered[:, :depth], right_ref[...], preferred_element_type=jnp.float32) + jnp.dot(
        ordered[:, depth:], right2_ref[...], preferred_element_type=jnp.float32
    )
    parts = sums.shape[1] // LANES
    first = LAST * 2 * slots
    for q in range(parts):
        columns = sums[:, q * LANES : (q + 1) * LANES]
        out_ref[pl.ds(q, first, stride=parts), :] = columns[2 * size - first :]
        out_ref[pl.ds(first * parts + q, 2 * size - first, stride=parts), :] = columns[: 2 * size - first]


def pack(marks, left):
    return pl.pallas_call(
        pack_kernel,
        out_shape=jax.ShapeDtypeStruct((16, PACKED_ROWS + LIST_ROWS, LANES), jnp.bfloat16),
        in_specs=[pl.BlockSpec(memory_space=pltpu.SMEM), pl.BlockSpec(memory_space=pltpu.VMEM)],
        out_specs=pl.BlockSpec(memory_space=pltpu.VMEM),
        scratch_shapes=[
            pltpu.VMEM(left.shape, jnp.bfloat16),
            pltpu.VMEM((2, PACKED_ROWS, LANES), jnp.bfloat16),
        ],
    )(marks, left)


def unpack_product(slots, facts, got, right, right2):
    depth, width = right.shape
    return pl.pallas_call(
        functools.partial(product_kernel, slots),
        out_shape=[
            jax.ShapeDtypeStruct((32 * slots * 2 * (width // LANES), LANES), jnp.float32),
            jax.ShapeDtypeStruct((1,), jnp.int32),
        ],
        in_specs=[pl.BlockSpec(memory_space=pltpu.VMEM)] * 4,
        out_specs=[pl.BlockSpec(memory_space=pltpu.VMEM), pl.BlockSpec(memory_space=pltpu.SMEM)],
        scratch_shapes=[
            pltpu.VMEM((512, 2 * depth), jnp.bfloat16),
            pltpu.VMEM((64 * slots, 2 * depth), jnp.bfloat16),
            pltpu.VMEM((24, LANES), jnp.int32),
            pltpu.SMEM((24, LANES), jnp.int32),
            pltpu.SemaphoreType.DMA,
        ],
        compiler_params=pltpu.CompilerParams(vmem_limit_bytes=24 * 2**20),
        cost_estimate=pl.CostEstimate(flops=2 * 512 * 2 * depth * width, bytes_accessed=4 * 2**20, transcendentals=0),
    )(facts, got, right, right2)


def spread_marks(marks):
    values = marks.astype(jnp.bfloat16)
    count_r, count_c = values.shape
    return jnp.broadcast_to(
        values[:, None, :, None], (count_r, ATOM_BLOCK, count_c, ATOM_BLOCK)
    ).reshape(count_r * ATOM_BLOCK, count_c * ATOM_BLOCK)


def dense_product(slots, core, owners, left, right, right2, occupancy):
    depth, width = right.shape
    kept = left * spread_marks(occupancy)
    halves = jnp.dot(row_order(), kept, preferred_element_type=jnp.float32).astype(jnp.bfloat16)
    sent = jnp.broadcast_to(halves.reshape(2, 1, HALF, depth), (2, 8, HALF, depth)).reshape(16, HALF, depth)
    panels = lax.all_to_all(sent, ("core", "zlo", "x"), 0, 0, tiled=True).reshape(2, 8 * HALF, depth)
    own = lax.dynamic_index_in_dim(panels, core, 0, keepdims=False)
    other = lax.dynamic_index_in_dim(panels, 1 - core, 0, keepdims=False)
    product = jnp.dot(own, right, preferred_element_type=jnp.float32) + jnp.dot(
        other, right2, preferred_element_type=jnp.float32
    )
    number = jnp.arange(8)
    owned = jnp.any(owners[:, None] == number[None, :], axis=0)
    before = jnp.sum(owned[:, None] & (number[:, None] < number[None, :]), axis=0)
    panel_of_slot = jnp.sum(jnp.where(owned[None, :] & (before[None, :] == number[:slots, None]), number[None, :], 0), axis=1)
    chosen = jnp.take(product.reshape(8, 32, 2 * width // LANES, LANES), panel_of_slot, axis=0)
    return lax.optimization_barrier(jnp.roll(chosen.transpose(1, 0, 2, 3), LAST, axis=0).reshape(-1, LANES))


def update(slab, chosen, sums):
    picked = jnp.sum(jnp.where(chosen.reshape(chosen.shape + (1,) * (sums.ndim - 1)), sums[None], 0.0), axis=1)
    return 1.5 * slab.astype(jnp.float32) - 0.5 * picked.reshape(slab.shape)


def body(left, right, occupancy, owners, slab):
    core = lax.axis_index("core")
    panels = jnp.arange(8)

    right2 = lax.ppermute(right, "core", [(0, 1), (1, 0)])
    packed, owners = lax.optimization_barrier((pack(occupancy, left), owners))
    got = lax.all_to_all(packed, ("core", "zlo", "x"), 0, 0, tiled=True)

    owned = jnp.any(owners[:, None] == panels[None, :], axis=0)
    number = jnp.sum(owned)
    slot_of_step = jnp.sum(owned[None, :] & (panels[None, :] < owners[:, None]), axis=1)

    facts = jnp.pad(jnp.concatenate([owners, core.reshape(1)]), (0, LANES - 9)).reshape(1, LANES)

    def reduced(slots):
        def branch():
            def to_wire(product):
                return (product * WIRE_SCALE).astype(WIRE).reshape(32, slots, TILE, LANES)

            product, flag = unpack_product(slots, facts, got, right, right2)
            parts = to_wire(product)
            parts = lax.switch(
                flag[0],
                [lambda: parts, lambda: to_wire(dense_product(slots, core, owners, left, right, right2, occupancy))],
            )
            came = lax.all_to_all(parts, ("zhi", "y"), 0, 0, axis_index_groups=[MEMBERS], tiled=True)
            sums = jnp.sum(came.astype(jnp.float32), axis=0) * (1.0 / WIRE_SCALE)
            return update(slab, slot_of_step[:, None] == jnp.arange(slots)[None, :], sums)

        return branch

    which = sum((number > slots).astype(jnp.int32) for slots in DISTINCT[:-1])
    return lax.switch(which, [reduced(slots) for slots in DISTINCT])


def solution(mesh):
    fine = Mesh(mesh.devices.reshape(4, 8, 2, 2, 4), ("zhi", "y", "core", "zlo", "x"))
    row, col = ("zhi", "y", "core"), ("zlo", "x")
    in_specs = (P(col, row), P(row, col), P(col, row), P(), P(None, row, col))
    out_specs = P(None, row, col)
    return jax.shard_map(body, mesh=fine, in_specs=in_specs, out_specs=out_specs, check_vma=False)
```

```python
import functools

import jax
import jax.numpy as jnp
from jax import lax
from jax.experimental import pallas as pl
from jax.experimental.pallas import tpu as pltpu
from jax.sharding import Mesh, PartitionSpec as P

ATOM_BLOCK = 64
PANEL_ROWS = 128
HALF = 64
SLOTS = 8
LANES = 128
TILE = 8
DISTINCT = (4, 5, 6, 8)
LAST = 4
MEMBERS = [(member - LAST) % 32 for member in range(32)]
COLUMNS = [6, 7, 0, 1, 2, 3, 4, 5]
SHARERS = [core * 8 + column for core in range(2) for column in COLUMNS]
PACKED_ROWS = SLOTS // 2 * 32
LIST_ROWS = 16
WIRE = jnp.float16
WIRE_SCALE = 128.0


def row_order():
    place = lax.broadcasted_iota(jnp.int32, (PANEL_ROWS, PANEL_ROWS), 0)
    row = lax.broadcasted_iota(jnp.int32, (PANEL_ROWS, PANEL_ROWS), 1)
    core, at, b = place // HALF, (place % HALF) // 2, place % 2
    return (row == at * 4 + core * 2 + b).astype(jnp.bfloat16)


def pack_kernel(marks_ref, left_ref, out_ref, rows, tiles):
    rows[...] = jnp.dot(row_order(), left_ref[...], preferred_element_type=jnp.float32).astype(jnp.bfloat16)
    tiles[...] = jnp.zeros_like(tiles)
    lane = lax.broadcasted_iota(jnp.int32, (32, LANES), 1)
    list_lane = lax.broadcasted_iota(jnp.int32, (LIST_ROWS, LANES), 1)
    block_rows, block_cols = marks_ref.shape
    count = jnp.int32(0)
    listed = jnp.zeros((LIST_ROWS, LANES), jnp.float32)
    for i in range(block_rows):
        for j in range(block_cols):
            kept = marks_ref[i, j] != 0
            slot = jnp.minimum(count, SLOTS - 1)
            fits = jnp.logical_and(kept, count < SLOTS)

            @pl.when(fits)
            def _(i=i, j=j, slot=slot):
                side = lax.rem(slot, 2)
                here = lane // ATOM_BLOCK == side
                at = pl.ds(pl.multiple_of(lax.div(slot, 2) * 32, 32), 32)
                for half in range(2):
                    block = rows[half * HALF + i * 32 : half * HALF + i * 32 + 32, j // 2 * LANES : (j // 2 + 1) * LANES]
                    turned = pltpu.roll(block, ATOM_BLOCK, 1)
                    placed = jnp.where(side == j % 2, block, turned)
                    tiles[half, at, :] = jnp.where(here, placed, tiles[half, at, :])

            mark = jnp.where(fits, 1.0, 0.0)
            listed = listed + jnp.where(list_lane == slot, mark * i, 0.0)
            listed = listed + jnp.where(list_lane == slot + 16, mark * j, 0.0)
            count = count + kept.astype(jnp.int32)
    listed = listed + jnp.where(list_lane == 32, count.astype(jnp.float32), 0.0)
    for to in range(out_ref.shape[0]):
        out_ref[to, :PACKED_ROWS, :] = tiles[to // 8]
        out_ref[to, PACKED_ROWS:, :] = listed.astype(jnp.bfloat16)


def destination_order(places, row_of_owners, slots):
    place = lax.broadcasted_iota(jnp.int32, (32 * slots, 1), 0)
    at = sum((place >= k * 2 * slots).astype(jnp.int32) for k in range(1, 16))
    slot, b = (place - at * (2 * slots)) // 2, place % 2
    wanted = at * 2 + b
    filled = jnp.int32(0)
    owners = [places[row_of_owners, t] for t in range(8)]
    for panel in range(8):
        owned = functools.reduce(jnp.logical_or, [owner == panel for owner in owners])
        wanted = wanted + jnp.where(slot == jnp.where(owned, filled, slots), panel * 32, 0)
        filled = filled + owned.astype(jnp.int32)
    row = lax.broadcasted_iota(jnp.int32, (32 * slots, 256), 1)
    return (row == wanted).astype(jnp.bfloat16)


def product_kernel(slots, facts_ref, got_ref, right_ref, right2_ref, out_ref, flag_ref, dense, ordered, lists, places, sem):
    sources = got_ref.shape[0]
    depth = right_ref.shape[0]
    lists[sources : sources + 1, :] = facts_ref[...]
    for source in range(sources):
        lists[source : source + 1, :] = got_ref[source, PACKED_ROWS : PACKED_ROWS + 1, :].astype(jnp.int32)
    copy = pltpu.make_async_copy(lists, places, sem)
    copy.start()
    dense[...] = jnp.zeros_like(dense)
    copy.wait()
    core = places[sources, 8]
    order = destination_order(places, sources, slots)
    side_of_lane = lax.broadcasted_iota(jnp.int32, (32, LANES), 1) // ATOM_BLOCK

    def put(source, first, slots_here):
        for slot in slots_here:
            i = places[source, slot]
            j = places[source, slot + 16]
            block = got_ref[source, slot // 2 * 32 : slot // 2 * 32 + 32, :]
            turned = pltpu.roll(block, ATOM_BLOCK, 1)
            side = lax.rem(j, 2)
            placed = jnp.where(side == slot % 2, block, turned)
            to_rows = pl.ds(pl.multiple_of(i * 256 + COLUMNS[source % 8] * 32, 32), 32)
            to_lanes = pl.ds(pl.multiple_of(first + lax.div(j, 2) * LANES, LANES), LANES)
            here = side_of_lane == jnp.where(slot < places[source, 32], side, 2)
            dense[to_rows, to_lanes] = jnp.where(here, placed, dense[to_rows, to_lanes])

    firsts = [jnp.where(core == source // 8, 0, depth) for source in range(sources)]
    for source in range(sources):
        put(source, firsts[source], range(SLOTS // 2))
    most = jnp.int32(0)
    for source in range(sources):
        most = jnp.maximum(most, places[source, 32])

        @pl.when(places[source, 32] > SLOTS // 2)
        def _(source=source):
            put(source, firsts[source], range(SLOTS // 2, SLOTS))

    flag_ref[0] = (most > SLOTS).astype(jnp.int32)

    size = 32 * slots
    for i in range(2):
        ordered[i * size : i * size + size, :] = jnp.dot(
            order, dense[i * 256 : i * 256 + 256, :], preferred_element_type=jnp.float32
        ).astype(jnp.bfloat16)
    sums = jnp.dot(ordered[:, :depth], right_ref[...], preferred_element_type=jnp.float32) + jnp.dot(
        ordered[:, depth:], right2_ref[...], preferred_element_type=jnp.float32
    )
    parts = sums.shape[1] // LANES
    first = LAST * 2 * slots
    for q in range(parts):
        columns = sums[:, q * LANES : (q + 1) * LANES]
        out_ref[pl.ds(q, first, stride=parts), :] = columns[2 * size - first :]
        out_ref[pl.ds(first * parts + q, 2 * size - first, stride=parts), :] = columns[: 2 * size - first]


def pack(marks, left):
    return pl.pallas_call(
        pack_kernel,
        out_shape=jax.ShapeDtypeStruct((16, PACKED_ROWS + LIST_ROWS, LANES), jnp.bfloat16),
        in_specs=[pl.BlockSpec(memory_space=pltpu.SMEM), pl.BlockSpec(memory_space=pltpu.VMEM)],
        out_specs=pl.BlockSpec(memory_space=pltpu.VMEM),
        scratch_shapes=[
            pltpu.VMEM(left.shape, jnp.bfloat16),
            pltpu.VMEM((2, PACKED_ROWS, LANES), jnp.bfloat16),
        ],
    )(marks, left)


def unpack_product(slots, facts, got, right, right2):
    depth, width = right.shape
    return pl.pallas_call(
        functools.partial(product_kernel, slots),
        out_shape=[
            jax.ShapeDtypeStruct((32 * slots * 2 * (width // LANES), LANES), jnp.float32),
            jax.ShapeDtypeStruct((1,), jnp.int32),
        ],
        in_specs=[pl.BlockSpec(memory_space=pltpu.VMEM)] * 4,
        out_specs=[pl.BlockSpec(memory_space=pltpu.VMEM), pl.BlockSpec(memory_space=pltpu.SMEM)],
        scratch_shapes=[
            pltpu.VMEM((512, 2 * depth), jnp.bfloat16),
            pltpu.VMEM((64 * slots, 2 * depth), jnp.bfloat16),
            pltpu.VMEM((24, LANES), jnp.int32),
            pltpu.SMEM((24, LANES), jnp.int32),
            pltpu.SemaphoreType.DMA,
        ],
        compiler_params=pltpu.CompilerParams(vmem_limit_bytes=24 * 2**20),
        cost_estimate=pl.CostEstimate(flops=2 * 512 * 2 * depth * width, bytes_accessed=4 * 2**20, transcendentals=0),
    )(facts, got, right, right2)


def spread_marks(marks):
    values = marks.astype(jnp.bfloat16)
    count_r, count_c = values.shape
    return jnp.broadcast_to(
        values[:, None, :, None], (count_r, ATOM_BLOCK, count_c, ATOM_BLOCK)
    ).reshape(count_r * ATOM_BLOCK, count_c * ATOM_BLOCK)


def dense_product(slots, core, owners, left, right, right2, occupancy):
    depth, width = right.shape
    kept = left * spread_marks(occupancy)
    halves = jnp.dot(row_order(), kept, preferred_element_type=jnp.float32).astype(jnp.bfloat16)
    sent = jnp.broadcast_to(halves.reshape(2, 1, HALF, depth), (2, 8, HALF, depth)).reshape(16, HALF, depth)
    panels = lax.all_to_all(sent, ("core", "zlo", "x"), 0, 0, tiled=True).reshape(2, 8 * HALF, depth)
    own = lax.dynamic_index_in_dim(panels, core, 0, keepdims=False)
    other = lax.dynamic_index_in_dim(panels, 1 - core, 0, keepdims=False)
    product = jnp.dot(own, right, preferred_element_type=jnp.float32) + jnp.dot(
        other, right2, preferred_element_type=jnp.float32
    )
    number = jnp.arange(8)
    owned = jnp.any(owners[:, None] == number[None, :], axis=0)
    before = jnp.sum(owned[:, None] & (number[:, None] < number[None, :]), axis=0)
    panel_of_slot = jnp.sum(jnp.where(owned[None, :] & (before[None, :] == number[:slots, None]), number[None, :], 0), axis=1)
    chosen = jnp.take(product.reshape(8, 32, 2 * width // LANES, LANES), panel_of_slot, axis=0)
    return lax.optimization_barrier(jnp.roll(chosen.transpose(1, 0, 2, 3), LAST, axis=0).reshape(-1, LANES))


def update(slab, chosen, sums):
    picked = jnp.sum(jnp.where(chosen.reshape(chosen.shape + (1,) * (sums.ndim - 1)), sums[None], 0.0), axis=1)
    return 1.5 * slab.astype(jnp.float32) - 0.5 * picked.reshape(slab.shape)


def body(left, right, occupancy, owners, slab):
    core = lax.axis_index("core")
    panels = jnp.arange(8)

    right2 = lax.ppermute(right, "core", [(0, 1), (1, 0)])
    packed, owners = lax.optimization_barrier((pack(occupancy, left), owners))
    got = lax.all_to_all(packed, ("core", "zlo", "x"), 0, 0, axis_index_groups=[SHARERS], tiled=True)

    owned = jnp.any(owners[:, None] == panels[None, :], axis=0)
    number = jnp.sum(owned)
    slot_of_step = jnp.sum(owned[None, :] & (panels[None, :] < owners[:, None]), axis=1)

    facts = jnp.pad(jnp.concatenate([owners, core.reshape(1)]), (0, LANES - 9)).reshape(1, LANES)

    def reduced(slots):
        def branch():
            def to_wire(product):
                return (product * WIRE_SCALE).astype(WIRE).reshape(32, slots, TILE, LANES)

            product, flag = unpack_product(slots, facts, got, right, right2)
            parts = to_wire(product)
            parts = lax.switch(
                flag[0],
                [lambda: parts, lambda: to_wire(dense_product(slots, core, owners, left, right, right2, occupancy))],
            )
            came = lax.all_to_all(parts, ("zhi", "y"), 0, 0, axis_index_groups=[MEMBERS], tiled=True)
            sums = jnp.sum(came.astype(jnp.float32), axis=0) * (1.0 / WIRE_SCALE)
            return update(slab, slot_of_step[:, None] == jnp.arange(slots)[None, :], sums)

        return branch

    which = sum((number > slots).astype(jnp.int32) for slots in DISTINCT[:-1])
    return lax.switch(which, [reduced(slots) for slots in DISTINCT])


def solution(mesh):
    fine = Mesh(mesh.devices.reshape(4, 8, 2, 2, 4), ("zhi", "y", "core", "zlo", "x"))
    row, col = ("zhi", "y", "core"), ("zlo", "x")
    in_specs = (P(col, row), P(row, col), P(col, row), P(), P(None, row, col))
    out_specs = P(None, row, col)
    return jax.shard_map(body, mesh=fine, in_specs=in_specs, out_specs=out_specs, check_vma=False)
```

```python
import functools

import jax
import jax.numpy as jnp
from jax import lax
from jax.experimental import pallas as pl
from jax.experimental.pallas import tpu as pltpu
from jax.sharding import Mesh, PartitionSpec as P

ATOM_BLOCK = 64
PANEL_ROWS = 128
HALF = 64
SLOTS = 8
LANES = 128
TILE = 8
DISTINCT = (5, 6, 8)
LAST = 4
MEMBERS = [(member - LAST) % 32 for member in range(32)]
COLUMNS = [6, 7, 0, 1, 2, 3, 4, 5]
SHARERS = [core * 8 + column for core in range(2) for column in COLUMNS]
PACKED_ROWS = SLOTS // 2 * 32
LIST_ROWS = 16
WIRE = jnp.float16
WIRE_SCALE = 128.0


def row_order():
    place = lax.broadcasted_iota(jnp.int32, (PANEL_ROWS, PANEL_ROWS), 0)
    row = lax.broadcasted_iota(jnp.int32, (PANEL_ROWS, PANEL_ROWS), 1)
    core, at, b = place // HALF, (place % HALF) // 2, place % 2
    return (row == at * 4 + core * 2 + b).astype(jnp.bfloat16)


def pack_kernel(marks_ref, left_ref, out_ref, rows, tiles):
    rows[...] = jnp.dot(row_order(), left_ref[...], preferred_element_type=jnp.float32).astype(jnp.bfloat16)
    tiles[...] = jnp.zeros_like(tiles)
    lane = lax.broadcasted_iota(jnp.int32, (32, LANES), 1)
    list_lane = lax.broadcasted_iota(jnp.int32, (LIST_ROWS, LANES), 1)
    block_rows, block_cols = marks_ref.shape
    count = jnp.int32(0)
    listed = jnp.zeros((LIST_ROWS, LANES), jnp.float32)
    for i in range(block_rows):
        for j in range(block_cols):
            kept = marks_ref[i, j] != 0
            slot = jnp.minimum(count, SLOTS - 1)
            fits = jnp.logical_and(kept, count < SLOTS)

            @pl.when(fits)
            def _(i=i, j=j, slot=slot):
                side = lax.rem(slot, 2)
                here = lane // ATOM_BLOCK == side
                at = pl.ds(pl.multiple_of(lax.div(slot, 2) * 32, 32), 32)
                for half in range(2):
                    block = rows[half * HALF + i * 32 : half * HALF + i * 32 + 32, j // 2 * LANES : (j // 2 + 1) * LANES]
                    turned = pltpu.roll(block, ATOM_BLOCK, 1)
                    placed = jnp.where(side == j % 2, block, turned)
                    tiles[half, at, :] = jnp.where(here, placed, tiles[half, at, :])

            mark = jnp.where(fits, 1.0, 0.0)
            listed = listed + jnp.where(list_lane == slot, mark * i, 0.0)
            listed = listed + jnp.where(list_lane == slot + 16, mark * j, 0.0)
            count = count + kept.astype(jnp.int32)
    listed = listed + jnp.where(list_lane == 32, count.astype(jnp.float32), 0.0)
    for to in range(out_ref.shape[0]):
        out_ref[to, :PACKED_ROWS, :] = tiles[to // 8]
        out_ref[to, PACKED_ROWS:, :] = listed.astype(jnp.bfloat16)


def destination_order(places, row_of_owners, slots):
    place = lax.broadcasted_iota(jnp.int32, (32 * slots, 1), 0)
    at = sum((place >= k * 2 * slots).astype(jnp.int32) for k in range(1, 16))
    slot, b = (place - at * (2 * slots)) // 2, place % 2
    wanted = at * 2 + b
    filled = jnp.int32(0)
    owners = [places[row_of_owners, t] for t in range(8)]
    for panel in range(8):
        owned = functools.reduce(jnp.logical_or, [owner == panel for owner in owners])
        wanted = wanted + jnp.where(slot == jnp.where(owned, filled, slots), panel * 32, 0)
        filled = filled + owned.astype(jnp.int32)
    row = lax.broadcasted_iota(jnp.int32, (32 * slots, 256), 1)
    return (row == wanted).astype(jnp.bfloat16)


def product_kernel(slots, facts_ref, got_ref, right_ref, right2_ref, out_ref, flag_ref, dense, ordered, lists, places, sem):
    sources = got_ref.shape[0]
    depth = right_ref.shape[0]
    lists[sources : sources + 1, :] = facts_ref[...]
    for source in range(sources):
        lists[source : source + 1, :] = got_ref[source, PACKED_ROWS:, :].astype(jnp.int32)[:1]
    copy = pltpu.make_async_copy(lists, places, sem)
    copy.start()
    dense[...] = jnp.zeros_like(dense)
    copy.wait()
    core = places[sources, 8]
    order = destination_order(places, sources, slots)
    side_of_lane = lax.broadcasted_iota(jnp.int32, (32, LANES), 1) // ATOM_BLOCK

    def put(source, first, slots_here):
        for slot in slots_here:
            i = places[source, slot]
            j = places[source, slot + 16]
            block = got_ref[source, slot // 2 * 32 : slot // 2 * 32 + 32, :]
            turned = pltpu.roll(block, ATOM_BLOCK, 1)
            side = lax.rem(j, 2)
            placed = jnp.where(side == slot % 2, block, turned)
            to_rows = pl.ds(pl.multiple_of(i * 256 + COLUMNS[source % 8] * 32, 32), 32)
            to_lanes = pl.ds(pl.multiple_of(first + lax.div(j, 2) * LANES, LANES), LANES)
            here = side_of_lane == jnp.where(slot < places[source, 32], side, 2)
            dense[to_rows, to_lanes] = jnp.where(here, placed, dense[to_rows, to_lanes])

    firsts = [jnp.where(core == source // 8, 0, depth) for source in range(sources)]
    for source in range(sources):
        put(source, firsts[source], range(SLOTS // 2))
    most = jnp.int32(0)
    for source in range(sources):
        most = jnp.maximum(most, places[source, 32])

        @pl.when(places[source, 32] > SLOTS // 2)
        def _(source=source):
            put(source, firsts[source], range(SLOTS // 2, SLOTS))

    flag_ref[0] = (most > SLOTS).astype(jnp.int32)

    size = 32 * slots
    for i in range(2):
        ordered[i * size : i * size + size, :] = jnp.dot(
            order, dense[i * 256 : i * 256 + 256, :], preferred_element_type=jnp.float32
        ).astype(jnp.bfloat16)
    sums = jnp.dot(ordered[:, :depth], right_ref[...], preferred_element_type=jnp.float32) + jnp.dot(
        ordered[:, depth:], right2_ref[...], preferred_element_type=jnp.float32
    )
    parts = sums.shape[1] // LANES
    first = LAST * 2 * slots
    for q in range(parts):
        columns = sums[:, q * LANES : (q + 1) * LANES]
        out_ref[pl.ds(q, first, stride=parts), :] = columns[2 * size - first :]
        out_ref[pl.ds(first * parts + q, 2 * size - first, stride=parts), :] = columns[: 2 * size - first]


def pack(marks, left):
    return pl.pallas_call(
        pack_kernel,
        out_shape=jax.ShapeDtypeStruct((16, PACKED_ROWS + LIST_ROWS, LANES), jnp.bfloat16),
        in_specs=[pl.BlockSpec(memory_space=pltpu.SMEM), pl.BlockSpec(memory_space=pltpu.VMEM)],
        out_specs=pl.BlockSpec(memory_space=pltpu.VMEM),
        scratch_shapes=[
            pltpu.VMEM(left.shape, jnp.bfloat16),
            pltpu.VMEM((2, PACKED_ROWS, LANES), jnp.bfloat16),
        ],
    )(marks, left)


def unpack_product(slots, facts, got, right, right2):
    depth, width = right.shape
    return pl.pallas_call(
        functools.partial(product_kernel, slots),
        out_shape=[
            jax.ShapeDtypeStruct((32 * slots * 2 * (width // LANES), LANES), jnp.float32),
            jax.ShapeDtypeStruct((1,), jnp.int32),
        ],
        in_specs=[pl.BlockSpec(memory_space=pltpu.VMEM)] * 4,
        out_specs=[pl.BlockSpec(memory_space=pltpu.VMEM), pl.BlockSpec(memory_space=pltpu.SMEM)],
        scratch_shapes=[
            pltpu.VMEM((512, 2 * depth), jnp.bfloat16),
            pltpu.VMEM((64 * slots, 2 * depth), jnp.bfloat16),
            pltpu.VMEM((24, LANES), jnp.int32),
            pltpu.SMEM((24, LANES), jnp.int32),
            pltpu.SemaphoreType.DMA,
        ],
        compiler_params=pltpu.CompilerParams(vmem_limit_bytes=24 * 2**20),
        cost_estimate=pl.CostEstimate(flops=2 * 512 * 2 * depth * width, bytes_accessed=4 * 2**20, transcendentals=0),
    )(facts, got, right, right2)


def spread_marks(marks):
    values = marks.astype(jnp.bfloat16)
    count_r, count_c = values.shape
    return jnp.broadcast_to(
        values[:, None, :, None], (count_r, ATOM_BLOCK, count_c, ATOM_BLOCK)
    ).reshape(count_r * ATOM_BLOCK, count_c * ATOM_BLOCK)


def dense_product(slots, core, owners, left, right, right2, occupancy):
    depth, width = right.shape
    kept = left * spread_marks(occupancy)
    halves = jnp.dot(row_order(), kept, preferred_element_type=jnp.float32).astype(jnp.bfloat16)
    sent = jnp.broadcast_to(halves.reshape(2, 1, HALF, depth), (2, 8, HALF, depth)).reshape(16, HALF, depth)
    panels = lax.all_to_all(sent, ("core", "zlo", "x"), 0, 0, tiled=True).reshape(2, 8 * HALF, depth)
    own = lax.dynamic_index_in_dim(panels, core, 0, keepdims=False)
    other = lax.dynamic_index_in_dim(panels, 1 - core, 0, keepdims=False)
    product = jnp.dot(own, right, preferred_element_type=jnp.float32) + jnp.dot(
        other, right2, preferred_element_type=jnp.float32
    )
    number = jnp.arange(8)
    owned = jnp.any(owners[:, None] == number[None, :], axis=0)
    before = jnp.sum(owned[:, None] & (number[:, None] < number[None, :]), axis=0)
    panel_of_slot = jnp.sum(jnp.where(owned[None, :] & (before[None, :] == number[:slots, None]), number[None, :], 0), axis=1)
    chosen = jnp.take(product.reshape(8, 32, 2 * width // LANES, LANES), panel_of_slot, axis=0)
    return lax.optimization_barrier(jnp.roll(chosen.transpose(1, 0, 2, 3), LAST, axis=0).reshape(-1, LANES))


def update(slab, chosen, sums):
    picked = jnp.sum(jnp.where(chosen.reshape(chosen.shape + (1,) * (sums.ndim - 1)), sums[None], 0.0), axis=1)
    return 1.5 * slab.astype(jnp.float32) - 0.5 * picked.reshape(slab.shape)


def body(left, right, occupancy, owners, slab):
    core = lax.axis_index("core")
    panels = jnp.arange(8)

    right2 = lax.ppermute(right, "core", [(0, 1), (1, 0)])
    packed, owners = lax.optimization_barrier((pack(occupancy, left), owners))
    got = lax.all_to_all(packed, ("core", "zlo", "x"), 0, 0, axis_index_groups=[SHARERS], tiled=True)

    owned = jnp.any(owners[:, None] == panels[None, :], axis=0)
    number = jnp.sum(owned)
    slot_of_step = jnp.sum(owned[None, :] & (panels[None, :] < owners[:, None]), axis=1)

    facts = jnp.pad(jnp.concatenate([owners, core.reshape(1)]), (0, LANES - 9)).reshape(1, LANES)

    def reduced(slots):
        def branch():
            def to_wire(product):
                return (product * WIRE_SCALE).astype(WIRE).reshape(32, slots, TILE, LANES)

            product, flag = unpack_product(slots, facts, got, right, right2)
            parts = to_wire(product)
            parts = lax.switch(
                flag[0],
                [lambda: parts, lambda: to_wire(dense_product(slots, core, owners, left, right, right2, occupancy))],
            )
            came = lax.all_to_all(parts, ("zhi", "y"), 0, 0, axis_index_groups=[MEMBERS], tiled=True)
            sums = jnp.sum(came.astype(jnp.float32), axis=0) * (1.0 / WIRE_SCALE)
            return update(slab, slot_of_step[:, None] == jnp.arange(slots)[None, :], sums)

        return branch

    which = sum((number > slots).astype(jnp.int32) for slots in DISTINCT[:-1])
    return lax.switch(which, [reduced(slots) for slots in DISTINCT])


def solution(mesh):
    fine = Mesh(mesh.devices.reshape(4, 8, 2, 2, 4), ("zhi", "y", "core", "zlo", "x"))
    row, col = ("zhi", "y", "core"), ("zlo", "x")
    in_specs = (P(col, row), P(row, col), P(col, row), P(), P(None, row, col))
    out_specs = P(None, row, col)
    return jax.shard_map(body, mesh=fine, in_specs=in_specs, out_specs=out_specs, check_vma=False)
```
